32 devices in a mesh: pipe: 2 (over core), expert: 16 (over z, y, x).
Axes of the slice: x: 2, y: 2, z: 4, core: 2. Of those that a mesh axis runs over, the one named last changes fastest.
Arguments:
- tokens: bfloat16 [2, 1792, 4096], P(None, 'expert'), may hold values from -6 to 6
- cotangent: bfloat16 [2, 1792, 4096], P(None, 'expert'), may hold values from -6 to 6
- expert_ids: int32 [2, 2, 1792, 2], P('pipe', None, 'expert'), may hold values from 0 to 15, all different within a row; in each aligned block of 112 rows (0 to 111, 112 to 223, ..., all dimensions but the last counted through in order) at most 17 rows name the same one
- gate_prob: float32 [2, 2, 1792, 2], P('pipe', None, 'expert'), may hold values from 0.25 to 1
- up_weight: bfloat16 [2, 16, 4096, 768], P('pipe', 'expert'), may hold values from -0.09375 to 0.09375
- down_weight: bfloat16 [2, 16, 768, 4096], P('pipe', 'expert'), may hold values from -0.21875 to 0.21875
Outputs:
- input_grad: bfloat16 [2, 2, 1792, 4096], P('pipe', None, 'expert')
- down_grad: bfloat16 [2, 16, 768, 4096], P('pipe', 'expert')
The draws below stay inside these ranges and needn't reach their ends.
Inputs may be any that keep to these rules, and one draw needn't show every extreme that they name: `expert_ids`: for each section and micro-batch, the 112 rows of one device name no expert more than 17 times, a bound that some block reaches; the two ids of a row differ.
All inputs are finite; a program needn't handle non-finite values.
Results may differ from the reference program's by a relative error of at most 0.015.
Values may be sent and summed in bfloat16 or wider, within the bound.
No kernel may reach another device: no remote copies, remote signals or barrier semaphores. Data moves between devices by JAX's collectives and lax.ppermute only.
A program may use at most 192 MiB of HBM per device.

```python
import math
import jax
import jax.numpy as jnp
import numpy as np
from jax import lax

D = 4096
FF = 768
MICRO = 2
TOK_DEV = 112
EXPERTS = 16
SECTIONS = 2
TOKENS = 1792
CAP = 17
N_EXPERT = 16


def steps_of(key, dims, shards, smallest, largest):
    gain = 1.0
    for axis_at, blocks in shards:
        heights = jax.random.uniform(jax.random.fold_in(jax.random.fold_in(key, 6), axis_at), (blocks,), jnp.float32, smallest / len(shards), largest / len(shards))
        gain = gain * jnp.repeat(jnp.exp(heights), dims[axis_at] // blocks).reshape((-1,) + (1,) * (len(dims) - 1 - axis_at))
    return gain


def deal_out(stream_key, own, number, rows, amount, top, most, slope):
    ranking = jax.random.permutation(stream_key, amount)
    heavy_load, common = shares(amount, rows * top, most, slope, True), shares(amount, rows * top, most, slope, False)
    places = jnp.arange(amount)

    def named(lengths, turn):
        used = int((lengths > 0).sum())
        fixed = max(1, used // 4)
        passed = fixed + (places - fixed + turn * (used - fixed)) % max(1, amount - fixed)
        return jnp.zeros((amount,), jnp.int32).at[ranking[jnp.where(places < fixed, places, passed)]].set(jnp.asarray(lengths, jnp.int32))

    lengths = jnp.where(number % 4 == 0, named(heavy_load, number // 4), named(common, number - number // 4 - 1))
    mixed = jax.random.permutation(jax.random.fold_in(own, 3), amount)
    source_of, taker = mixed[0:amount // 2 * 2:2], mixed[1:amount // 2 * 2:2]
    room = jnp.minimum(lengths[source_of] - 1, most - lengths[taker]) // 2
    room = jnp.where((source_of == ranking[0]) | (taker == ranking[0]) | (lengths[taker] == 0), 0, jnp.maximum(room, 0))
    passed = jax.random.randint(jax.random.fold_in(own, 4), (amount // 2,), 0, 1 << 20) % (room + 1)
    lengths = lengths.at[source_of].add(-passed).at[taker].add(passed)
    labels = jnp.searchsorted(jnp.cumsum(lengths), jnp.arange(rows * top), side="right").astype(jnp.int32)
    table = labels.reshape(top, rows).T
    table = table[jax.random.permutation(jax.random.fold_in(own, 1), rows)]
    turn = jax.random.randint(jax.random.fold_in(own, 2), (rows, 1), 0, top)
    return jnp.take_along_axis(table, (jnp.arange(top)[None, :] + turn) % top, axis=1)


def shares(count, total, reach, skew, full):
    portions = [(1 << 20) // math.isqrt(standing ** skew) + 1 for standing in range(1, count + 1)]
    largest = reach if full else min(reach, max(-(-total // count), total * portions[0] // sum(portions)))
    least = 1 if total - largest >= count - 1 else 0
    holding, spare = [largest] + [least] * (count - 1), total - largest - least * (count - 1)
    while spare > 0:
        free = [i for i in range(1, count) if holding[i] < largest] or [i for i in range(1, count) if holding[i] < reach]
        whole, budget = sum([portions[i] for i in free]), spare
        for i in free:
            more = min(reach - holding[i], max(1, budget * portions[i] // whole), spare)
            holding[i] = holding[i] + more
            spare = spare - more
    return np.array(holding)


def bell_draw(rng, dims, scale, reach, shards=(), kind=jnp.bfloat16):
    result = jax.random.normal(rng, dims, jnp.float32) * scale
    if len(shards) > 0:
        result = steps_of(rng, dims, shards, -0.22, 0.18) * result
    return jnp.clip(result, min=-reach, max=reach).astype(kind)


def setup_inputs(seed: int = 0) -> dict:
    keys = jax.random.split(jax.random.key(seed), 7)
    tokens = bell_draw(keys[0], (MICRO, TOKENS, D), 1.0, 6.0, ((1, 16),))
    cotangent = bell_draw(keys[1], (MICRO, TOKENS, D), 1.0, 6.0, ((1, 16),))
    expert_ids_keys = jax.random.split(jax.random.fold_in(keys[2], 1), SECTIONS * MICRO * TOKENS // TOK_DEV)
    expert_ids_turns = jax.random.permutation(jax.random.fold_in(keys[2], 3), SECTIONS * MICRO * TOKENS // TOK_DEV)
    expert_ids = jax.vmap(lambda own, number: deal_out(jax.random.fold_in(keys[2], 2), own, number, TOK_DEV, EXPERTS, 2, CAP, 2))(expert_ids_keys, expert_ids_turns).reshape((SECTIONS, MICRO, TOKENS, 2))
    gate_prob = jnp.clip(0.25 + 0.75 * jax.random.uniform(keys[3], (SECTIONS, MICRO, TOKENS, 2), jnp.float32) ** steps_of(keys[3], (SECTIONS, MICRO, TOKENS, 2), ((0, 2), (2, 16)), -0.2, 0.2), 0.25, 1.0)
    up_weight = bell_draw(keys[4], (SECTIONS, EXPERTS, D, FF), D ** -0.5, 0.09375, ((0, 2), (1, 16)))
    down_weight = bell_draw(keys[5], (SECTIONS, EXPERTS, FF, D), FF ** -0.5, 0.21875, ((0, 2), (1, 16)))
    return dict(tokens=tokens, cotangent=cotangent, expert_ids=expert_ids, gate_prob=gate_prob, up_weight=up_weight, down_weight=down_weight)


EPSILON = 1e-06
ROOT_HALF = 0.7071067811865476
INV_ROOT_TAU = 0.3989422804014327

def gelu_value(values):
    return 0.5 * values * (1.0 + jax.scipy.special.erf(values * ROOT_HALF))

def gelu_slope(values):
    return 0.5 * (1.0 + jax.scipy.special.erf(values * ROOT_HALF)) + values * jnp.exp(-0.5 * values * values) * INV_ROOT_TAU

def normalize(carried):
    widened = carried.astype(jnp.float32)
    inverse_rms = lax.rsqrt(lax.optimization_barrier(jnp.mean(widened * widened, axis=-1, keepdims=True)) + EPSILON)
    return ((widened * inverse_rms).astype(jnp.bfloat16), inverse_rms)

def norm_back(carried, inverse_rms, upstream):
    widened = carried.astype(jnp.float32)
    inner = lax.optimization_barrier(jnp.mean(widened * upstream, axis=-1, keepdims=True))
    return inverse_rms * upstream - widened * (inverse_rms * inverse_rms * inverse_rms) * inner

def slot_targets(chosen_ids, expert_count, capacity):
    flattened = chosen_ids.reshape(-1).astype(jnp.int32)
    onehot = (flattened[:, None] == jnp.arange(expert_count, dtype=jnp.int32)[None, :]).astype(jnp.int32)
    before = jnp.cumsum(onehot, axis=0) - onehot
    slot_index = lax.optimization_barrier(jnp.sum(before * onehot, axis=1))
    return flattened * capacity + slot_index

def route_table(chosen_ids, blocks, expert_count, capacity):
    local_slot = jax.vmap(lambda block_ids: slot_targets(block_ids, expert_count, capacity))(chosen_ids.reshape(blocks, -1, 2))
    source = jnp.arange(blocks, dtype=jnp.int32)[:, None]
    expert_index = local_slot // capacity
    return (expert_index * (blocks * capacity) + source * capacity + local_slot % capacity).reshape(-1).astype(jnp.int32)

def expert_forward(operands):
    row_block, up_matrix, down_matrix = operands
    hidden = jnp.dot(row_block, up_matrix, preferred_element_type=jnp.float32)
    activated = gelu_value(hidden).astype(jnp.bfloat16)
    return jnp.dot(activated, down_matrix, preferred_element_type=jnp.float32).astype(jnp.bfloat16)

def expert_backward(operands):
    row_block, grad_block, up_matrix, down_matrix = operands
    hidden = jnp.dot(row_block, up_matrix, preferred_element_type=jnp.float32)
    activated = gelu_value(hidden).astype(jnp.bfloat16)
    back_act = jnp.dot(grad_block, down_matrix.T, preferred_element_type=jnp.float32)
    back_hidden = (back_act * gelu_slope(hidden)).astype(jnp.bfloat16)
    back_pick = jnp.dot(back_hidden, up_matrix.T, preferred_element_type=jnp.float32).astype(jnp.bfloat16)
    down_part = jnp.dot(activated.T, grad_block, preferred_element_type=jnp.float32).astype(jnp.bfloat16)
    return (back_pick, down_part)

def reference(tokens, cotangent, expert_ids, gate_prob, up_weight, down_weight):
    blocks = N_EXPERT
    capacity = CAP
    span_rows = blocks * capacity
    slot_total = EXPERTS * span_rows
    token_count = tokens.shape[1]
    feature_count = tokens.shape[2]
    owner_base = jnp.arange(2 * token_count, dtype=jnp.int32) // 2

    def prepare(carried, section, number):
        normed, inverse_rms = normalize(carried)
        targets = route_table(expert_ids[section, number], blocks, EXPERTS, capacity)
        owner_row = jnp.full((slot_total,), token_count, jnp.int32).at[targets].set(owner_base)
        extended = jnp.concatenate([normed, jnp.zeros((1, feature_count), normed.dtype)], axis=0)
        gathered = extended[owner_row].reshape(EXPERTS, span_rows, feature_count)
        return (gathered, targets, inverse_rms)
    current = [tokens[number] for number in range(MICRO)]
    saved = []
    for section in range(SECTIONS):
        saved.append(current)
        following = []
        for number in range(MICRO):
            carried = current[number]
            gathered, targets, inverse_rms = prepare(carried, section, number)
            answers = lax.map(expert_forward, (gathered, up_weight[section], down_weight[section]))
            picked = answers.reshape(slot_total, feature_count)[targets].reshape(token_count, 2, feature_count)
            mixed_sum = carried.astype(jnp.float32) + lax.optimization_barrier(jnp.sum(gate_prob[section, number][:, :, None] * picked.astype(jnp.float32), axis=1))
            following.append(mixed_sum.astype(jnp.bfloat16))
        current = following
    input_grads = [None] * SECTIONS
    down_grads = [None] * SECTIONS
    incoming = [cotangent[number] for number in range(MICRO)]
    for section in reversed(range(SECTIONS)):
        normed_rows = []
        grad_rows = []
        target_list = []
        scale_list = []
        for number in range(MICRO):
            carried = saved[section][number]
            gathered, targets, inverse_rms = prepare(carried, section, number)
            weighted = (gate_prob[section, number][:, :, None] * incoming[number].astype(jnp.float32)[:, None, :]).astype(jnp.bfloat16)
            grad_buffer = jnp.zeros((slot_total, feature_count), jnp.bfloat16).at[targets].set(weighted.reshape(2 * token_count, feature_count))
            normed_rows.append(gathered)
            grad_rows.append(grad_buffer.reshape(EXPERTS, span_rows, feature_count))
            target_list.append(targets)
            scale_list.append(inverse_rms)
        back_picks, down_part = lax.map(expert_backward, (jnp.concatenate(normed_rows, axis=1), jnp.concatenate(grad_rows, axis=1), up_weight[section], down_weight[section]))
        previous_list = []
        for number in range(MICRO):
            block_back = back_picks[:, number * span_rows:(number + 1) * span_rows].reshape(slot_total, feature_count)
            picked = block_back[target_list[number]].reshape(token_count, 2, feature_count)
            back_normed = lax.optimization_barrier(jnp.sum(picked.astype(jnp.float32), axis=1))
            previous = incoming[number].astype(jnp.float32) + norm_back(saved[section][number], scale_list[number], back_normed)
            previous_list.append(previous.astype(jnp.bfloat16))
        input_grads[section] = jnp.stack(previous_list, axis=0)
        down_grads[section] = down_part
        incoming = previous_list
    return (jnp.stack(input_grads, axis=0), jnp.stack(down_grads, axis=0))
```

```python
import functools

import jax
import jax.numpy as jnp
from jax import lax
from jax.experimental import pallas as pl
from jax.experimental.pallas import tpu as pltpu
from jax.sharding import PartitionSpec as P

EPSILON = 1e-06
ROOT_HALF = 0.7071067811865476
INV_ROOT_TAU = 0.3989422804014327
BF16 = jnp.bfloat16
F32 = jnp.float32
FEATURE_BLOCKS = 8
SLOT_TILE = 16
VMEM_BYTES = 56 * 1024 * 1024


class Sizes:
    def __init__(self, experts, rows, features, hidden):
        self.experts, self.rows, self.features, self.hidden = experts, rows, features, hidden
        self.capacity = 5 * rows // (2 * experts)
        self.lanes = features // FEATURE_BLOCKS
        self.tiled = self.capacity // SLOT_TILE * SLOT_TILE
        self.rest = self.capacity - self.tiled
        self.tiled_rows = experts * self.tiled
        self.rest_rows = experts * self.rest
        self.slots = experts * self.capacity
        self.message = (experts, FEATURE_BLOCKS * self.capacity, self.lanes)


def iota(shape, axis):
    return lax.broadcasted_iota(jnp.int32, shape, axis)


def dot(left, right):
    return jnp.dot(left, right, preferred_element_type=F32)


def dot_last(left, right):
    return lax.dot_general(left, right, (((1,), (1,)), ((), ())), preferred_element_type=F32)


def gelu_value(values):
    return 0.5 * values * (1.0 + lax.erf(values * ROOT_HALF))


def gelu_slope(values):
    return (
        0.5 * (1.0 + lax.erf(values * ROOT_HALF))
        + values * jnp.exp(-0.5 * values * values) * INV_ROOT_TAU
    )


def halves(values):
    high = values.astype(BF16)
    return high, (values - high.astype(F32)).astype(BF16)


def slot_parts(sizes):
    parts = []
    if sizes.tiled:
        parts.append((sizes.tiled, 0))
    if sizes.rest:
        parts.append((sizes.rest, sizes.tiled))
    return parts


def expansion(sizes, width):
    count = sizes.experts * width
    shape = (count, sizes.experts)
    first = iota(shape, 1) * width
    row = iota(shape, 0)
    return ((row >= first) & (row < first + width)).astype(BF16)


def expansion_across(sizes, width):
    count = sizes.experts * width
    shape = (sizes.experts, count)
    first = iota(shape, 0) * width
    column = iota(shape, 1)
    return ((column >= first) & (column < first + width)).astype(BF16)


def slots_by_token(sizes, table_across, gated):
    rows = sizes.rows
    names = iota((sizes.experts, rows), 0).astype(F32)
    first = table_across[0:1, :] == names
    second = table_across[1:2, :] == names
    chosen = jnp.where(first | second, 1.0, 0.0)
    earlier = (iota((rows, rows), 0) < iota((rows, rows), 1)).astype(BF16)
    rank = jnp.where(chosen > 0.0, dot(chosen.astype(BF16), earlier), -1.0).astype(BF16)
    if gated:
        gate = jnp.where(first, table_across[2:3, :], 0.0) + jnp.where(
            second, table_across[3:4, :], 0.0
        )
        high, low = halves(gate)
    ones, highs, lows = [], [], []
    for width, start in slot_parts(sizes):
        spread = expansion(sizes, width)
        ranks = dot(spread, rank)
        place = iota(ranks.shape, 0) % width + start
        here = ranks == place.astype(F32)
        if gated:
            highs.append(jnp.where(here, dot(spread, high), 0.0).astype(BF16))
            lows.append(jnp.where(here, dot(spread, low), 0.0).astype(BF16))
        else:
            ones.append(jnp.where(here, 1.0, 0.0).astype(BF16))
    if gated:
        return jnp.concatenate(highs, axis=0), jnp.concatenate(lows, axis=0)
    return jnp.concatenate(ones, axis=0)


def tokens_by_slot(sizes, table, gated):
    rows = sizes.rows
    names = iota((rows, sizes.experts), 1).astype(F32)
    first = table[:, 0:1] == names
    second = table[:, 1:2] == names
    chosen = jnp.where(first | second, 1.0, 0.0)
    earlier = (iota((rows, rows), 1) < iota((rows, rows), 0)).astype(BF16)
    rank = jnp.where(chosen > 0.0, dot(earlier, chosen.astype(BF16)), -1.0).astype(BF16)
    if gated:
        gate = jnp.where(first, table[:, 2:3], 0.0) + jnp.where(second, table[:, 3:4], 0.0)
        high, low = halves(gate)
    ones, highs, lows = [], [], []
    for width, start in slot_parts(sizes):
        spread = expansion_across(sizes, width)
        ranks = dot(rank, spread)
        place = iota(ranks.shape, 1) % width + start
        here = ranks == place.astype(F32)
        if gated:
            highs.append(jnp.where(here, dot(high, spread), 0.0).astype(BF16))
            lows.append(jnp.where(here, dot(low, spread), 0.0).astype(BF16))
        else:
            ones.append(jnp.where(here, 1.0, 0.0).astype(BF16))
    if gated:
        return jnp.concatenate(highs, axis=1), jnp.concatenate(lows, axis=1)
    return jnp.concatenate(ones, axis=1)


def write_tiled(sizes, message, block, values):
    if sizes.tiled:
        message[:, block * sizes.tiled : (block + 1) * sizes.tiled, :] = (
            values[: sizes.tiled_rows].astype(BF16).reshape(sizes.experts, sizes.tiled, sizes.lanes)
        )
    return values[sizes.tiled_rows :].astype(BF16)


def rest_places(sizes, block):
    shape = (sizes.rest_rows * FEATURE_BLOCKS, sizes.rest_rows)
    return (iota(shape, 0) == iota(shape, 1) * FEATURE_BLOCKS + block).astype(BF16)


def rest_places_across(sizes, block):
    shape = (sizes.rest_rows, sizes.rest_rows * FEATURE_BLOCKS)
    return (iota(shape, 1) == iota(shape, 0) * FEATURE_BLOCKS + block).astype(BF16)


def write_message(sizes, message, block_values):
    rest = None
    for block in range(FEATURE_BLOCKS):
        other = write_tiled(sizes, message, block, block_values(block))
        if sizes.rest:
            part = dot(rest_places(sizes, block), other)
            rest = part if rest is None else rest + part
    if sizes.rest:
        first = FEATURE_BLOCKS * sizes.tiled
        message[:, first:, :] = rest.reshape(
            sizes.experts, FEATURE_BLOCKS * sizes.rest, sizes.lanes
        ).astype(BF16)


def read_rest(sizes, message):
    if not sizes.rest:
        return None
    first = FEATURE_BLOCKS * sizes.tiled
    return (
        message[:, first:, :]
        .astype(F32)
        .reshape(sizes.rest_rows * FEATURE_BLOCKS, sizes.lanes)
        .astype(BF16)
    )


def read_block(sizes, message, rest, block):
    parts = []
    if sizes.tiled:
        parts.append(
            message[:, block * sizes.tiled : (block + 1) * sizes.tiled, :].reshape(
                sizes.tiled_rows, sizes.lanes
            )
        )
    if sizes.rest:
        parts.append(dot(rest_places_across(sizes, block), rest).astype(BF16))
    return jnp.concatenate(parts, axis=0)


def span(sizes, block):
    return slice(block * sizes.lanes, (block + 1) * sizes.lanes)


def inverse_rms(sizes, read):
    total = jnp.zeros((sizes.rows, 1), F32)
    for block in range(FEATURE_BLOCKS):
        wide = read(block).astype(F32)
        total = total + jnp.sum(wide * wide, axis=1, keepdims=True)
    return lax.rsqrt(total / sizes.features + EPSILON)


def send_normed(sizes, carried, across, message):
    scale = inverse_rms(sizes, lambda block: carried[:, span(sizes, block)])
    select = slots_by_token(sizes, across, False)

    def values(block):
        normed = (carried[:, span(sizes, block)].astype(F32) * scale).astype(BF16)
        return dot(select, normed)

    write_message(sizes, message, values)


def send_weighted(sizes, incoming, across, message):
    high, low = slots_by_token(sizes, across, True)

    def values(block):
        rows = incoming[:, span(sizes, block)]
        return dot(high, rows) + dot(low, rows)

    write_message(sizes, message, values)


def first_kernel(sizes, which, carried, across, message):
    send_normed(sizes, carried.at[0], across, message)


def cotangent_kernel(sizes, which, incoming, across, message):
    send_weighted(sizes, incoming.at[0], across, message)


def middle_kernel(sizes, which, before, answer, table, across, carried, message):
    high, low = tokens_by_slot(sizes, table, True)
    rest = read_rest(sizes, answer)
    for block in range(FEATURE_BLOCKS):
        rows = read_block(sizes, answer, rest, block)
        mixed = before[0, :, span(sizes, block)].astype(F32) + (dot(high, rows) + dot(low, rows))
        carried[:, span(sizes, block)] = mixed.astype(BF16)
    send_normed(sizes, carried, across, message)


def norm_back(sizes, carried, incoming, answer, table, upstream, result):
    select = tokens_by_slot(sizes, table, False)
    rest = read_rest(sizes, answer)
    inner = jnp.zeros((sizes.rows, 1), F32)
    squares = jnp.zeros((sizes.rows, 1), F32)
    for block in range(FEATURE_BLOCKS):
        here = span(sizes, block)
        back = dot(select, read_block(sizes, answer, rest, block))
        wide = carried[:, here].astype(F32)
        upstream[:, here] = back
        inner = inner + jnp.sum(wide * back, axis=1, keepdims=True)
        squares = squares + jnp.sum(wide * wide, axis=1, keepdims=True)
    scale = lax.rsqrt(squares / sizes.features + EPSILON)
    pull = scale * scale * scale * (inner / sizes.features)
    for block in range(FEATURE_BLOCKS):
        here = span(sizes, block)
        wide = carried[:, here].astype(F32)
        result[:, here] = (
            incoming[:, here].astype(F32) + (scale * upstream[:, here] - wide * pull)
        ).astype(BF16)


def turn_kernel(
    sizes, which, carried, incoming, answer, table, across, result, message, upstream
):
    norm_back(sizes, carried, incoming.at[0], answer, table, upstream, result)
    send_weighted(sizes, result, across, message)


def last_kernel(sizes, which, carried, incoming, answer, table, result, upstream):
    norm_back(sizes, carried.at[0], incoming, answer, table, upstream, result)


def fetch(which, wanted, own, other, place, semaphores, pieces):
    def begin(source):
        for number, piece in enumerate(pieces):
            pltpu.make_async_copy(
                source.at[piece], place.at[piece], semaphores.at[number]
            ).start()

    @pl.when(which[0] == wanted)
    def _():
        begin(own)

    @pl.when(which[0] != wanted)
    def _():
        begin(other)

    def wait(number):
        piece = pieces[number]
        pltpu.make_async_copy(own.at[piece], place.at[piece], semaphores.at[number]).wait()

    return wait


def up_pieces(sizes):
    return [
        (pl.ds(block * sizes.lanes, sizes.lanes), slice(None)) for block in range(FEATURE_BLOCKS)
    ]


def down_pieces(sizes):
    return [
        (slice(None), pl.ds(block * sizes.lanes, sizes.lanes)) for block in range(FEATURE_BLOCKS)
    ]


def forward_kernel(
    sizes, section, which, received, up, up_other, down, down_other,
    hidden_out, activated_out, message, up_here, down_here, up_done, down_done,
):
    up_wait = fetch(which, section, up, up_other, up_here, up_done, up_pieces(sizes))
    down_wait = fetch(which, section, down, down_other, down_here, down_done, down_pieces(sizes))
    rest = read_rest(sizes, received)
    hidden = jnp.zeros((sizes.slots, sizes.hidden), F32)
    for block in range(FEATURE_BLOCKS):
        rows = read_block(sizes, received, rest, block)
        up_wait(block)
        hidden = hidden + dot(rows, up_here[span(sizes, block), :])
    hidden_out[...] = hidden
    activated = gelu_value(hidden).astype(BF16)
    activated_out[...] = activated

    def values(block):
        down_wait(block)
        return dot(activated, down_here[:, span(sizes, block)])

    write_message(sizes, message, values)


def hidden_back_kernel(
    sizes, section, which, received, down, down_other, back_out, down_here, down_done
):
    down_wait = fetch(which, section, down, down_other, down_here, down_done, down_pieces(sizes))
    rest = read_rest(sizes, received)
    back = jnp.zeros((sizes.slots, sizes.hidden), F32)
    for block in range(FEATURE_BLOCKS):
        rows = read_block(sizes, received, rest, block)
        down_wait(block)
        back = back + dot_last(rows, down_here[:, span(sizes, block)])
    back_out[...] = back


def back_message(sizes, back_hidden, up_here, message):
    write_message(
        sizes, message, lambda block: dot_last(back_hidden, up_here[span(sizes, block), :])
    )


def turn_expert_kernel(
    sizes, section, which, received, back, up, up_other,
    activated_out, message, up_here, up_done,
):
    up_wait = fetch(which, section, up, up_other, up_here, up_done, up_pieces(sizes))
    rest = read_rest(sizes, received)
    hidden = jnp.zeros((sizes.slots, sizes.hidden), F32)
    for block in range(FEATURE_BLOCKS):
        rows = read_block(sizes, received, rest, block)
        up_wait(block)
        hidden = hidden + dot(rows, up_here[span(sizes, block), :])
    activated_out[...] = gelu_value(hidden).astype(BF16)
    back_hidden = (back[...] * gelu_slope(hidden)).astype(BF16)
    back_message(sizes, back_hidden, up_here, message)


def backward_kernel(
    sizes, section, which, received, hidden, up, up_other, down, down_other,
    message, up_here, down_here, up_done, down_done,
):
    down_wait = fetch(which, section, down, down_other, down_here, down_done, down_pieces(sizes))
    up_wait = fetch(which, section, up, up_other, up_here, up_done, up_pieces(sizes))
    slope = gelu_slope(hidden[...])
    rest = read_rest(sizes, received)
    back = jnp.zeros((sizes.slots, sizes.hidden), F32)
    for block in range(FEATURE_BLOCKS):
        rows = read_block(sizes, received, rest, block)
        down_wait(block)
        back = back + dot_last(rows, down_here[:, span(sizes, block)])
    back_hidden = (back * slope).astype(BF16)
    for block in range(FEATURE_BLOCKS):
        up_wait(block)
    back_message(sizes, back_hidden, up_here, message)


def down_grad_kernel(
    sizes, which, activated_0, grad_0, activated_1, grad_1, activated_far, grad_far,
    result, activated_here, grad_here, done,
):
    everything = (slice(None), slice(None))
    whole = (slice(None), slice(None), slice(None))
    activated_wait = fetch(
        which, 0, activated_0, activated_1, activated_here, done.at[pl.ds(0, 1)], [everything]
    )
    grad_wait = fetch(which, 0, grad_0, grad_1, grad_here, done.at[pl.ds(1, 1)], [whole])
    activated_wait(0)
    grad_wait(0)
    near, far = activated_here[...], activated_far[...]
    rest_near, rest_far = read_rest(sizes, grad_here), read_rest(sizes, grad_far)
    over_rows = (((0,), (0,)), ((), ()))
    for block in range(FEATURE_BLOCKS):
        rows_near = read_block(sizes, grad_here, rest_near, block)
        rows_far = read_block(sizes, grad_far, rest_far, block)
        total = lax.dot_general(near, rows_near, over_rows, preferred_element_type=F32)
        total = total + lax.dot_general(far, rows_far, over_rows, preferred_element_type=F32)
        result[:, span(sizes, block)] = total.astype(BF16)


VMEM = pl.BlockSpec(memory_space=pltpu.VMEM)
HBM = pl.BlockSpec(memory_space=pl.ANY)


def call(kernel, name, which, operands, specs, outs, scratch=()):
    def chosen(shape):
        return pl.BlockSpec((1,) + shape[1:], lambda step, pick: (pick[0], 0, 0))

    in_specs = [
        chosen(operand.shape) if spec == "clip" else spec for operand, spec in zip(operands, specs)
    ]
    return pl.pallas_call(
        kernel,
        name=name,
        grid_spec=pltpu.PrefetchScalarGridSpec(
            num_scalar_prefetch=1,
            grid=(1,),
            in_specs=in_specs,
            out_specs=[VMEM] * len(outs),
            scratch_shapes=list(scratch),
        ),
        out_shape=[jax.ShapeDtypeStruct(shape, kind) for shape, kind in outs],
        compiler_params=pltpu.CompilerParams(vmem_limit_bytes=VMEM_BYTES),
    )(which, *operands)


def exchange(message):
    return lax.all_to_all(message, "expert", split_axis=0, concat_axis=0, tiled=True)


def shards(tokens, cotangent, expert_ids, gate_prob, up_weight, down_weight):
    core = lax.axis_index("pipe")
    rows, features = tokens.shape[1], tokens.shape[2]
    hidden = up_weight.shape[3]
    sizes = Sizes(lax.axis_size("expert"), rows, features, hidden)
    swap = [(0, 1), (1, 0)]
    which = jnp.reshape(core, (1,)).astype(jnp.int32)

    tables = jnp.concatenate([expert_ids[0].astype(F32), gate_prob[0]], axis=-1)
    mine = lax.dynamic_index_in_dim(tables, core, 0, keepdims=False)
    theirs = lax.dynamic_index_in_dim(tables, 1 - core, 0, keepdims=False)
    theirs = lax.ppermute(theirs, "pipe", swap)
    table_0 = jnp.where(core == 0, mine, theirs)
    table_1 = jnp.where(core == 0, theirs, mine)
    across_0, across_1 = table_0.T, table_1.T

    up, down = up_weight[0, 0], down_weight[0, 0]
    up_other = lax.ppermute(up, "pipe", swap)
    down_other = lax.ppermute(down, "pipe", swap)

    up_scratch = pltpu.VMEM((features, hidden), BF16)
    down_scratch = pltpu.VMEM((hidden, features), BF16)
    done_scratch = pltpu.SemaphoreType.DMA((FEATURE_BLOCKS,))
    upstream_scratch = pltpu.VMEM((rows, features), F32)
    message = (sizes.message, BF16)
    home_rows = ((rows, features), BF16)
    activated = ((sizes.slots, hidden), BF16)
    wide_hidden = ((sizes.slots, hidden), F32)

    def kernel(body, *more):
        return functools.partial(body, sizes, *more)

    (out_0,) = call(
        kernel(first_kernel), "send_tokens", which, [tokens, across_0], ["clip", VMEM], [message]
    )
    in_0 = exchange(out_0)
    (grad_out_1,) = call(
        kernel(cotangent_kernel), "send_cotangent", which, [cotangent, across_1],
        ["clip", VMEM], [message],
    )
    grad_in_1 = exchange(grad_out_1)
    hidden_0, activated_0, answer_0 = call(
        kernel(forward_kernel, 0), "expert_forward", which,
        [in_0, up, up_other, down, down_other], [VMEM, HBM, HBM, HBM, HBM],
        [wide_hidden, activated, message],
        [up_scratch, down_scratch, done_scratch, done_scratch],
    )
    returned_0 = exchange(answer_0)
    carried_1, out_1 = call(
        kernel(middle_kernel), "combine_send", which,
        [tokens, returned_0, table_0, across_1], ["clip", VMEM, VMEM, VMEM], [home_rows, message],
    )
    in_1 = exchange(out_1)
    (back_1,) = call(
        kernel(hidden_back_kernel, 1), "hidden_back", which,
        [grad_in_1, down, down_other], [VMEM, HBM, HBM], [wide_hidden],
        [down_scratch, done_scratch],
    )
    activated_1, picks_1 = call(
        kernel(turn_expert_kernel, 1), "expert_turn", which,
        [in_1, back_1, up, up_other], [VMEM, VMEM, HBM, HBM], [activated, message],
        [up_scratch, done_scratch],
    )
    back_home_1 = exchange(picks_1)
    grad_1, grad_out_0 = call(
        kernel(turn_kernel), "norm_back_send", which,
        [carried_1, cotangent, back_home_1, table_1, across_0],
        [VMEM, "clip", VMEM, VMEM, VMEM], [home_rows, message], [upstream_scratch],
    )
    grad_in_0 = exchange(grad_out_0)
    (picks_0,) = call(
        kernel(backward_kernel, 0), "expert_backward", which,
        [grad_in_0, hidden_0, up, up_other, down, down_other],
        [VMEM, VMEM, HBM, HBM, HBM, HBM], [message],
        [up_scratch, down_scratch, done_scratch, done_scratch],
    )
    back_home_0 = exchange(picks_0)

    to_first, to_second = [(1, 0)], [(0, 1)]
    activated_far = jnp.where(
        core == 0,
        lax.ppermute(activated_0, "pipe", to_first),
        lax.ppermute(activated_1, "pipe", to_second),
    )
    grad_far = jnp.where(
        core == 0,
        lax.ppermute(grad_in_0, "pipe", to_first),
        lax.ppermute(grad_in_1, "pipe", to_second),
    )
    (down_grad,) = call(
        kernel(down_grad_kernel), "down_grad", which,
        [activated_0, grad_in_0, activated_1, grad_in_1, activated_far, grad_far],
        [HBM, HBM, HBM, HBM, VMEM, VMEM], [((hidden, features), BF16)],
        [
            pltpu.VMEM((sizes.slots, hidden), BF16),
            pltpu.VMEM(sizes.message, BF16),
            pltpu.SemaphoreType.DMA((2,)),
        ],
    )

    (grad_0,) = call(
        kernel(last_kernel), "norm_back_last", which,
        [tokens, grad_1, back_home_0, table_0], ["clip", VMEM, VMEM, VMEM], [home_rows],
        [upstream_scratch],
    )
    far_1 = lax.ppermute(grad_1, "pipe", to_second)
    far_0 = lax.ppermute(grad_0, "pipe", to_first)
    input_grad = jnp.where(
        core == 0, jnp.stack([grad_0, far_0]), jnp.stack([far_1, grad_1])
    )
    return input_grad[None], down_grad[None, None]


def solution(mesh):
    placed = (
        P(None, "expert", None),
        P(None, "expert", None),
        P("pipe", None, "expert", None),
        P("pipe", None, "expert", None),
        P("pipe", "expert", None, None),
        P("pipe", "expert", None, None),
    )
    return jax.shard_map(
        shards,
        mesh=mesh,
        in_specs=placed,
        out_specs=(P("pipe", None, "expert", None), P("pipe", "expert", None, None)),
        check_vma=False,
    )
```

```python
import functools

import jax
import jax.numpy as jnp
from jax import lax
from jax.experimental import pallas as pl
from jax.experimental.pallas import tpu as pltpu
from jax.sharding import PartitionSpec as P

EPSILON = 1e-06
ROOT_HALF = 0.7071067811865476
INV_ROOT_TAU = 0.3989422804014327
BF16 = jnp.bfloat16
F32 = jnp.float32
FEATURE_BLOCKS = 8
SLOT_TILE = 16
VMEM_BYTES = 20 * 1024 * 1024


class Sizes:
    def __init__(self, experts, rows, features, hidden):
        self.experts, self.rows, self.features, self.hidden = experts, rows, features, hidden
        self.capacity = 5 * rows // (2 * experts)
        self.lanes = features // FEATURE_BLOCKS
        self.tiled = self.capacity // SLOT_TILE * SLOT_TILE
        self.rest = self.capacity - self.tiled
        self.tiled_rows = experts * self.tiled
        self.rest_rows = experts * self.rest
        self.slots = experts * self.capacity
        self.message = (experts, FEATURE_BLOCKS * self.capacity, self.lanes)


def iota(shape, axis):
    return lax.broadcasted_iota(jnp.int32, shape, axis)


def dot(left, right):
    return jnp.dot(left, right, preferred_element_type=F32)


def dot_last(left, right):
    return lax.dot_general(left, right, (((1,), (1,)), ((), ())), preferred_element_type=F32)


def gelu_value(values):
    return 0.5 * values * (1.0 + lax.erf(values * ROOT_HALF))


def gelu_slope(values):
    return (
        0.5 * (1.0 + lax.erf(values * ROOT_HALF))
        + values * jnp.exp(-0.5 * values * values) * INV_ROOT_TAU
    )


def halves(values):
    high = values.astype(BF16)
    return high, (values - high.astype(F32)).astype(BF16)


def slot_parts(sizes):
    parts = []
    if sizes.tiled:
        parts.append((sizes.tiled, 0))
    if sizes.rest:
        parts.append((sizes.rest, sizes.tiled))
    return parts


def expansion(sizes, width):
    count = sizes.experts * width
    shape = (count, sizes.experts)
    first = iota(shape, 1) * width
    row = iota(shape, 0)
    return ((row >= first) & (row < first + width)).astype(BF16)


def expansion_across(sizes, width):
    count = sizes.experts * width
    shape = (sizes.experts, count)
    first = iota(shape, 0) * width
    column = iota(shape, 1)
    return ((column >= first) & (column < first + width)).astype(BF16)


def slots_by_token(sizes, table_across, gated):
    rows = sizes.rows
    names = iota((sizes.experts, rows), 0).astype(F32)
    first = table_across[0:1, :] == names
    second = table_across[1:2, :] == names
    chosen = jnp.where(first | second, 1.0, 0.0)
    earlier = (iota((rows, rows), 0) < iota((rows, rows), 1)).astype(BF16)
    rank = jnp.where(chosen > 0.0, dot(chosen.astype(BF16), earlier), -1.0).astype(BF16)
    if gated:
        gate = jnp.where(first, table_across[2:3, :], 0.0) + jnp.where(
            second, table_across[3:4, :], 0.0
        )
        high, low = halves(gate)
    ones, highs, lows = [], [], []
    for width, start in slot_parts(sizes):
        spread = expansion(sizes, width)
        ranks = dot(spread, rank)
        place = iota(ranks.shape, 0) % width + start
        here = ranks == place.astype(F32)
        if gated:
            highs.append(jnp.where(here, dot(spread, high), 0.0).astype(BF16))
            lows.append(jnp.where(here, dot(spread, low), 0.0).astype(BF16))
        else:
            ones.append(jnp.where(here, 1.0, 0.0).astype(BF16))
    if gated:
        return jnp.concatenate(highs, axis=0), jnp.concatenate(lows, axis=0)
    return jnp.concatenate(ones, axis=0)


def tokens_by_slot(sizes, table, gated):
    rows = sizes.rows
    names = iota((rows, sizes.experts), 1).astype(F32)
    first = table[:, 0:1] == names
    second = table[:, 1:2] == names
    chosen = jnp.where(first | second, 1.0, 0.0)
    earlier = (iota((rows, rows), 1) < iota((rows, rows), 0)).astype(BF16)
    rank = jnp.where(chosen > 0.0, dot(earlier, chosen.astype(BF16)), -1.0).astype(BF16)
    if gated:
        gate = jnp.where(first, table[:, 2:3], 0.0) + jnp.where(second, table[:, 3:4], 0.0)
        high, low = halves(gate)
    ones, highs, lows = [], [], []
    for width, start in slot_parts(sizes):
        spread = expansion_across(sizes, width)
        ranks = dot(rank, spread)
        place = iota(ranks.shape, 1) % width + start
        here = ranks == place.astype(F32)
        if gated:
            highs.append(jnp.where(here, dot(high, spread), 0.0).astype(BF16))
            lows.append(jnp.where(here, dot(low, spread), 0.0).astype(BF16))
        else:
            ones.append(jnp.where(here, 1.0, 0.0).astype(BF16))
    if gated:
        return jnp.concatenate(highs, axis=1), jnp.concatenate(lows, axis=1)
    return jnp.concatenate(ones, axis=1)


def write_tiled(sizes, message, block, values):
    if sizes.tiled:
        message[:, block * sizes.tiled : (block + 1) * sizes.tiled, :] = (
            values[: sizes.tiled_rows].astype(BF16).reshape(sizes.experts, sizes.tiled, sizes.lanes)
        )
    return values[sizes.tiled_rows :].astype(BF16)


def rest_places(sizes, block):
    shape = (sizes.rest_rows * FEATURE_BLOCKS, sizes.rest_rows)
    return (iota(shape, 0) == iota(shape, 1) * FEATURE_BLOCKS + block).astype(BF16)


def rest_places_across(sizes, block):
    shape = (sizes.rest_rows, sizes.rest_rows * FEATURE_BLOCKS)
    return (iota(shape, 1) == iota(shape, 0) * FEATURE_BLOCKS + block).astype(BF16)


def write_message(sizes, message, block_values):
    rest = None
    for block in range(FEATURE_BLOCKS):
        other = write_tiled(sizes, message, block, block_values(block))
        if sizes.rest:
            part = dot(rest_places(sizes, block), other)
            rest = part if rest is None else rest + part
    if sizes.rest:
        first = FEATURE_BLOCKS * sizes.tiled
        message[:, first:, :] = rest.reshape(
            sizes.experts, FEATURE_BLOCKS * sizes.rest, sizes.lanes
        ).astype(BF16)


def read_rest(sizes, message):
    if not sizes.rest:
        return None
    first = FEATURE_BLOCKS * sizes.tiled
    return (
        message[:, first:, :]
        .astype(F32)
        .reshape(sizes.rest_rows * FEATURE_BLOCKS, sizes.lanes)
        .astype(BF16)
    )


def read_block(sizes, message, rest, block):
    parts = []
    if sizes.tiled:
        parts.append(
            message[:, block * sizes.tiled : (block + 1) * sizes.tiled, :].reshape(
                sizes.tiled_rows, sizes.lanes
            )
        )
    if sizes.rest:
        parts.append(dot(rest_places_across(sizes, block), rest).astype(BF16))
    return jnp.concatenate(parts, axis=0)


def span(sizes, block):
    return slice(block * sizes.lanes, (block + 1) * sizes.lanes)


def inverse_rms(sizes, read):
    total = jnp.zeros((sizes.rows, 1), F32)
    for block in range(FEATURE_BLOCKS):
        wide = read(block).astype(F32)
        total = total + jnp.sum(wide * wide, axis=1, keepdims=True)
    return lax.rsqrt(total / sizes.features + EPSILON)


def clip_copy(pick, clips, place, done):
    copy = pltpu.make_async_copy(clips.at[pick[0]], place, done)
    copy.start()
    return copy


def first_kernel(sizes, pick, clips, across, message, clip, done):
    clip_copy(pick, clips, clip, done.at[0]).wait()
    send_normed(sizes, clip, across, message)


def cotangent_kernel(sizes, pick, clips, across, message, clip, done):
    clip_copy(pick, clips, clip, done.at[0]).wait()
    send_weighted(sizes, clip, across, message)


def send_normed(sizes, carried, across, message):
    scale = inverse_rms(sizes, lambda block: carried[:, span(sizes, block)])
    select = slots_by_token(sizes, across[...], False)

    def values(block):
        normed = (carried[:, span(sizes, block)].astype(F32) * scale).astype(BF16)
        return dot(select, normed)

    write_message(sizes, message, values)


def send_weighted(sizes, incoming, across, message):
    high, low = slots_by_token(sizes, across[...], True)

    def values(block):
        rows = incoming[:, span(sizes, block)]
        return dot(high, rows) + dot(low, rows)

    write_message(sizes, message, values)


def middle_kernel(sizes, pick, clips, answer, table, across, carried, message, before, done):
    copy = clip_copy(pick, clips, before, done.at[0])
    high, low = tokens_by_slot(sizes, table[...], True)
    rest = read_rest(sizes, answer)
    copy.wait()
    for block in range(FEATURE_BLOCKS):
        rows = read_block(sizes, answer, rest, block)
        mixed = before[:, span(sizes, block)].astype(F32) + (dot(high, rows) + dot(low, rows))
        carried[:, span(sizes, block)] = mixed.astype(BF16)
    send_normed(sizes, carried, across, message)


def norm_back(sizes, carried, incoming, answer, table, result, upstream, copies):
    select = tokens_by_slot(sizes, table[...], False)
    rest = read_rest(sizes, answer)
    copies[0].wait()
    inner = jnp.zeros((sizes.rows, 1), F32)
    squares = jnp.zeros((sizes.rows, 1), F32)
    for block in range(FEATURE_BLOCKS):
        here = span(sizes, block)
        back = dot(select, read_block(sizes, answer, rest, block))
        wide = carried[:, here].astype(F32)
        upstream[:, here] = back
        inner = inner + jnp.sum(wide * back, axis=1, keepdims=True)
        squares = squares + jnp.sum(wide * wide, axis=1, keepdims=True)
    scale = lax.rsqrt(squares / sizes.features + EPSILON)
    pull = scale * scale * scale * (inner / sizes.features)
    copies[1].wait()
    for block in range(FEATURE_BLOCKS):
        here = span(sizes, block)
        wide = carried[:, here].astype(F32)
        result[:, here] = (
            incoming[:, here].astype(F32) + (scale * upstream[:, here] - wide * pull)
        ).astype(BF16)


def last_kernel(
    sizes, pick, clips, incoming, answer, table, far, result, whole, upstream, clip, grad, done
):
    copies = [
        clip_copy(pick, clips, clip, done.at[0]),
        pltpu.make_async_copy(incoming, grad, done.at[1]),
    ]
    copies[1].start()
    near_first = pltpu.make_async_copy(result, whole.at[0], done.at[2])
    far_first = pltpu.make_async_copy(far, whole.at[0], done.at[2])
    near_last = pltpu.make_async_copy(incoming, whole.at[1], done.at[3])

    @pl.when(pick[0] != 0)
    def _():
        far_first.start()
        near_last.start()

    norm_back(sizes, clip, grad, answer, table, result, upstream, copies)

    @pl.when(pick[0] == 0)
    def _():
        near_first.start()
        near_first.wait()

    @pl.when(pick[0] != 0)
    def _():
        far_first.wait()
        near_last.wait()


def turn_kernel(
    sizes, pick, carried, clips, answer, table, across, result, message, upstream, held, grad, done
):
    copies = [
        pltpu.make_async_copy(carried, held, done.at[0]),
        clip_copy(pick, clips, grad, done.at[1]),
    ]
    copies[0].start()
    norm_back(sizes, held, grad, answer, table, result, upstream, copies)
    send_weighted(sizes, result, across, message)


def through_up(sizes, received, up):
    rest = read_rest(sizes, received)
    hidden = jnp.zeros((sizes.slots, sizes.hidden), F32)
    for block in range(FEATURE_BLOCKS):
        rows = read_block(sizes, received, rest, block)
        hidden = hidden + dot(rows, up[span(sizes, block), :])
    return hidden


def through_down_back(sizes, received, down):
    rest = read_rest(sizes, received)
    back = jnp.zeros((sizes.slots, sizes.hidden), F32)
    for block in range(FEATURE_BLOCKS):
        rows = read_block(sizes, received, rest, block)
        back = back + dot_last(rows, down[:, span(sizes, block)])
    return back


def back_message(sizes, back_hidden, up, message):
    write_message(sizes, message, lambda block: dot_last(back_hidden, up[span(sizes, block), :]))


def forward_kernel(sizes, received, up, down, hidden_out, activated_out, message):
    hidden = through_up(sizes, received, up)
    hidden_out[...] = hidden
    activated = gelu_value(hidden).astype(BF16)
    activated_out[...] = activated
    write_message(sizes, message, lambda block: dot(activated, down[:, span(sizes, block)]))


def hidden_back_kernel(sizes, received, down, back_out):
    back_out[...] = through_down_back(sizes, received, down)


def turn_expert_kernel(sizes, received, back, up, activated_out, message):
    hidden = through_up(sizes, received, up)
    activated_out[...] = gelu_value(hidden).astype(BF16)
    back_hidden = (back[...] * gelu_slope(hidden)).astype(BF16)
    back_message(sizes, back_hidden, up, message)


def backward_kernel(sizes, received, hidden, up, down, message):
    slope = gelu_slope(hidden[...])
    back = through_down_back(sizes, received, down)
    back_message(sizes, (back * slope).astype(BF16), up, message)


def choose(pick, wanted, sources, places, semaphores):
    count = len(places)

    def begin(chosen):
        for number in range(count):
            pltpu.make_async_copy(chosen[number], places[number], semaphores.at[number]).start()

    @pl.when(pick[0] == wanted)
    def _():
        begin(sources[:count])

    @pl.when(pick[0] != wanted)
    def _():
        begin(sources[count:])

    for number in range(count):
        pltpu.make_async_copy(sources[number], places[number], semaphores.at[number]).wait()


def weights_kernel(pick, up, down, up_other, down_other, up_0, down_0, up_1, down_1, done):
    mine, others = (up, down), (up_other, down_other)
    choose(pick, 0, mine + others + others + mine, (up_0, down_0, up_1, down_1), done)


def assemble_kernel(pick, far, mine, whole, done):
    @pl.when(pick[0] == 0)
    def _():
        copy = pltpu.make_async_copy(far, whole.at[1], done.at[0])
        copy.start()
        copy.wait()


def down_grad_kernel(sizes, pick, *refs):
    sources, result, here, done = refs[:8], refs[8], refs[9:13], refs[13]
    choose(pick, 0, sources, here, done)
    near, near_grad, far, far_grad = here
    rest_near, rest_far = read_rest(sizes, near_grad), read_rest(sizes, far_grad)
    over_rows = (((0,), (0,)), ((), ()))
    for block in range(FEATURE_BLOCKS):
        rows_near = read_block(sizes, near_grad, rest_near, block)
        rows_far = read_block(sizes, far_grad, rest_far, block)
        total = lax.dot_general(near[...], rows_near, over_rows, preferred_element_type=F32)
        total = total + lax.dot_general(far[...], rows_far, over_rows, preferred_element_type=F32)
        result[:, span(sizes, block)] = total.astype(BF16)


VMEM = pl.BlockSpec(memory_space=pltpu.VMEM)
SMEM = pl.BlockSpec(memory_space=pltpu.SMEM)
HBM = pl.BlockSpec(memory_space=pltpu.HBM)


def call(kernel, name, operands, outs, scratch=(), specs=None, out_specs=None, aliases=None):
    return pl.pallas_call(
        kernel,
        name=name,
        in_specs=specs or [VMEM] * len(operands),
        out_specs=out_specs or [VMEM] * len(outs),
        out_shape=[
            jax.ShapeDtypeStruct(*out) if isinstance(out, tuple) else out for out in outs
        ],
        scratch_shapes=list(scratch),
        input_output_aliases=aliases or {},
        compiler_params=pltpu.CompilerParams(vmem_limit_bytes=VMEM_BYTES),
    )(*operands)


def exchange(message):
    return lax.all_to_all(message, "expert", split_axis=0, concat_axis=0, tiled=True)


def shards(tokens, cotangent, expert_ids, gate_prob, up_weight, down_weight):
    core = lax.axis_index("pipe")
    rows, features = tokens.shape[1], tokens.shape[2]
    hidden = up_weight.shape[3]
    sizes = Sizes(lax.axis_size("expert"), rows, features, hidden)
    swap = [(0, 1), (1, 0)]
    pick = jnp.reshape(core, (1,)).astype(jnp.int32)

    tables = jnp.concatenate([expert_ids[0].astype(F32), gate_prob[0]], axis=-1).swapaxes(1, 2)
    mine = lax.dynamic_index_in_dim(tables, core, 0, keepdims=False)
    theirs = lax.dynamic_index_in_dim(tables, 1 - core, 0, keepdims=False)
    theirs = lax.ppermute(theirs, "pipe", swap)
    across_0 = jnp.where(core == 0, mine, theirs)
    across_1 = jnp.where(core == 0, theirs, mine)
    table_0, table_1 = across_0.T, across_1.T
    up, down, theirs = lax.optimization_barrier((up_weight[0, 0], down_weight[0, 0], theirs))
    up_other = lax.ppermute(up, "pipe", swap)
    down_other = lax.ppermute(down, "pipe", swap)

    upstream_scratch = pltpu.VMEM((rows, features), F32)
    message = (sizes.message, BF16)
    home_rows = ((rows, features), BF16)
    activated = ((sizes.slots, hidden), BF16)
    wide_hidden = ((sizes.slots, hidden), F32)
    rows_scratch = pltpu.VMEM(*home_rows)
    up_shape, down_shape = ((features, hidden), BF16), ((hidden, features), BF16)

    def kernel(body, *more):
        return functools.partial(body, sizes, *more)

    def done(count):
        return pltpu.SemaphoreType.DMA((count,))

    up_0, down_0, up_1, down_1 = call(
        weights_kernel, "weights", [pick, up, down, up_other, down_other],
        [up_shape, down_shape] * 2, [done(4)], [SMEM] + [HBM] * 4, [HBM] * 4,
    )
    (out_0,) = call(
        kernel(first_kernel), "send_tokens", [pick, tokens, across_0], [message],
        [rows_scratch, done(1)], [SMEM, HBM, VMEM],
    )
    in_0 = exchange(out_0)
    (grad_out_1,) = call(
        kernel(cotangent_kernel), "send_cotangent", [pick, cotangent, across_1], [message],
        [rows_scratch, done(1)], [SMEM, HBM, VMEM],
    )
    grad_out_1, in_0 = lax.optimization_barrier((grad_out_1, in_0))
    grad_in_1 = exchange(grad_out_1)
    hidden_0, activated_0, answer_0 = call(
        kernel(forward_kernel), "expert_forward", [in_0, up_0, down_0],
        [wide_hidden, activated, message],
    )
    answer_0, grad_in_1 = lax.optimization_barrier((answer_0, grad_in_1))
    returned_0 = exchange(answer_0)
    (back_1,) = call(kernel(hidden_back_kernel), "hidden_back", [grad_in_1, down_1], [wide_hidden])
    returned_0, back_1 = lax.optimization_barrier((returned_0, back_1))
    carried_1, out_1 = call(
        kernel(middle_kernel), "combine_send", [pick, tokens, returned_0, table_0, across_1],
        [home_rows, message], [rows_scratch, done(1)], [SMEM, HBM, VMEM, VMEM, VMEM],
    )
    in_1 = exchange(out_1)
    activated_1, picks_1 = call(
        kernel(turn_expert_kernel), "expert_turn", [in_1, back_1, up_1], [activated, message]
    )
    back_home_1 = exchange(picks_1)
    grad_1, grad_out_0 = call(
        kernel(turn_kernel), "norm_back_send",
        [pick, carried_1, cotangent, back_home_1, table_1, across_0],
        [home_rows, message], [upstream_scratch, rows_scratch, rows_scratch, done(2)],
        [SMEM, HBM, HBM, VMEM, VMEM, VMEM],
    )
    grad_in_0 = exchange(grad_out_0)
    (picks_0,) = call(
        kernel(backward_kernel), "expert_backward", [grad_in_0, hidden_0, up_0, down_0], [message]
    )
    back_home_0 = exchange(picks_0)

    to_first, to_second = [(1, 0)], [(0, 1)]
    operands = []
    for near, way in (
        ([activated_0, grad_in_0], to_first), ([activated_1, grad_in_1], to_second)
    ):
        operands += near + [lax.ppermute(array, "pipe", way) for array in near]
    (down_grad,) = call(
        kernel(down_grad_kernel), "down_grad", [pick] + operands, [((hidden, features), BF16)],
        [pltpu.VMEM(*activated), pltpu.VMEM(*message)] * 2 + [pltpu.SemaphoreType.DMA((4,))],
        [SMEM] + [HBM] * 8,
    )
    far_1 = lax.ppermute(grad_1, "pipe", to_second)
    down_grad, far_1, back_home_0 = lax.optimization_barrier((down_grad, far_1, back_home_0))
    held = (tokens.shape, BF16)
    grad_0, input_grad = call(
        kernel(last_kernel), "norm_back_last", [pick, tokens, grad_1, back_home_0, table_0, far_1],
        [home_rows, held], [upstream_scratch, rows_scratch, rows_scratch, done(4)],
        [SMEM, HBM, HBM, VMEM, VMEM, HBM], [VMEM, HBM],
    )
    far_0 = lax.ppermute(grad_0, "pipe", to_first)
    (input_grad,) = call(
        assemble_kernel, "assemble", [pick, far_0, input_grad], [held], [pltpu.SemaphoreType.DMA((1,))],
        [SMEM, HBM, HBM], [HBM], {2: 0},
    )
    return input_grad[None], down_grad[None, None]


def solution(mesh):
    placed = (
        P(None, "expert", None),
        P(None, "expert", None),
        P("pipe", None, "expert", None),
        P("pipe", None, "expert", None),
        P("pipe", "expert", None, None),
        P("pipe", "expert", None, None),
    )
    return jax.shard_map(
        shards,
        mesh=mesh,
        in_specs=placed,
        out_specs=(P("pipe", None, "expert", None), P("pipe", "expert", None, None)),
        check_vma=False,
    )
```

```python
import functools

import jax
import jax.numpy as jnp
from jax import lax
from jax.experimental import pallas as pl
from jax.experimental.pallas import tpu as pltpu
from jax.sharding import PartitionSpec as P

EPSILON = 1e-06
ROOT_HALF = 0.7071067811865476
INV_ROOT_TAU = 0.3989422804014327
BF16 = jnp.bfloat16
F32 = jnp.float32
FEATURE_BLOCKS = 8
PLANES = 4
SLOT_TILE = 16
VMEM_BYTES = 20 * 1024 * 1024
WHOLE_VMEM_BYTES = 60 * 1024 * 1024


class Sizes:
    def __init__(self, experts, rows, features, hidden):
        self.experts, self.rows, self.features, self.hidden = experts, rows, features, hidden
        self.capacity = 5 * rows // (2 * experts)
        self.lanes = features // FEATURE_BLOCKS
        self.tiled = self.capacity // SLOT_TILE * SLOT_TILE
        self.rest = self.capacity - self.tiled
        self.tiled_rows = experts * self.tiled
        self.rest_rows = experts * self.rest
        self.slots = experts * self.capacity
        self.message = (experts, FEATURE_BLOCKS * self.capacity, self.lanes)
        self.in_plane = experts // PLANES


def iota(shape, axis):
    return lax.broadcasted_iota(jnp.int32, shape, axis)


def dot(left, right):
    return jnp.dot(left, right, preferred_element_type=F32)


def dot_last(left, right):
    return lax.dot_general(left, right, (((1,), (1,)), ((), ())), preferred_element_type=F32)


def gelu_value(values):
    return 0.5 * values * (1.0 + lax.erf(values * ROOT_HALF))


def gelu_slope(values):
    return (
        0.5 * (1.0 + lax.erf(values * ROOT_HALF))
        + values * jnp.exp(-0.5 * values * values) * INV_ROOT_TAU
    )


def halves(values):
    high = values.astype(BF16)
    return high, (values - high.astype(F32)).astype(BF16)


def slot_parts(sizes):
    parts = []
    if sizes.tiled:
        parts.append((sizes.tiled, 0))
    if sizes.rest:
        parts.append((sizes.rest, sizes.tiled))
    return parts


def expansion(sizes, width):
    count = sizes.experts * width
    shape = (count, sizes.experts)
    first = iota(shape, 1) * width
    row = iota(shape, 0)
    return ((row >= first) & (row < first + width)).astype(BF16)


def expansion_across(sizes, width):
    count = sizes.experts * width
    shape = (sizes.experts, count)
    first = iota(shape, 0) * width
    column = iota(shape, 1)
    return ((column >= first) & (column < first + width)).astype(BF16)


def slots_by_token(sizes, table_across, gated, base=0):
    rows = sizes.rows
    names = (iota((sizes.experts, rows), 0) ^ base).astype(F32)
    first = table_across[0:1, :] == names
    second = table_across[1:2, :] == names
    chosen = jnp.where(first | second, 1.0, 0.0)
    earlier = (iota((rows, rows), 0) < iota((rows, rows), 1)).astype(BF16)
    rank = jnp.where(chosen > 0.0, dot(chosen.astype(BF16), earlier), -1.0).astype(BF16)
    if gated:
        gate = jnp.where(first, table_across[2:3, :], 0.0) + jnp.where(
            second, table_across[3:4, :], 0.0
        )
        high, low = halves(gate)
    ones, highs, lows = [], [], []
    for width, start in slot_parts(sizes):
        spread = expansion(sizes, width)
        ranks = dot(spread, rank)
        place = iota(ranks.shape, 0) % width + start
        here = ranks == place.astype(F32)
        if gated:
            highs.append(jnp.where(here, dot(spread, high), 0.0).astype(BF16))
            lows.append(jnp.where(here, dot(spread, low), 0.0).astype(BF16))
        else:
            ones.append(jnp.where(here, 1.0, 0.0).astype(BF16))
    if gated:
        return jnp.concatenate(highs, axis=0), jnp.concatenate(lows, axis=0)
    return jnp.concatenate(ones, axis=0)


def tokens_by_slot(sizes, table, gated):
    rows = sizes.rows
    names = iota((rows, sizes.experts), 1).astype(F32)
    first = table[:, 0:1] == names
    second = table[:, 1:2] == names
    chosen = jnp.where(first | second, 1.0, 0.0)
    earlier = (iota((rows, rows), 1) < iota((rows, rows), 0)).astype(BF16)
    rank = jnp.where(chosen > 0.0, dot(earlier, chosen.astype(BF16)), -1.0).astype(BF16)
    if gated:
        gate = jnp.where(first, table[:, 2:3], 0.0) + jnp.where(second, table[:, 3:4], 0.0)
        high, low = halves(gate)
    ones, highs, lows = [], [], []
    for width, start in slot_parts(sizes):
        spread = expansion_across(sizes, width)
        ranks = dot(rank, spread)
        place = iota(ranks.shape, 1) % width + start
        here = ranks == place.astype(F32)
        if gated:
            highs.append(jnp.where(here, dot(high, spread), 0.0).astype(BF16))
            lows.append(jnp.where(here, dot(low, spread), 0.0).astype(BF16))
        else:
            ones.append(jnp.where(here, 1.0, 0.0).astype(BF16))
    if gated:
        return jnp.concatenate(highs, axis=1), jnp.concatenate(lows, axis=1)
    return jnp.concatenate(ones, axis=1)


def rest_places(sizes, block):
    shape = (sizes.rest_rows * FEATURE_BLOCKS, sizes.rest_rows)
    return (iota(shape, 0) == iota(shape, 1) * FEATURE_BLOCKS + block).astype(BF16)


def rest_places_across(sizes, block):
    shape = (sizes.rest_rows, sizes.rest_rows * FEATURE_BLOCKS)
    return (iota(shape, 1) == iota(shape, 0) * FEATURE_BLOCKS + block).astype(BF16)


def write_pieces(sizes, pieces, block_values):
    tile, each = sizes.tiled, sizes.experts // len(pieces)
    rest = None
    for block in range(FEATURE_BLOCKS):
        values = block_values(block)
        if tile:
            for number, piece in enumerate(pieces):
                rows = values[number * each * tile : (number + 1) * each * tile].astype(BF16)
                piece[:, block * tile : (block + 1) * tile, :] = rows.reshape(
                    each, tile, sizes.lanes
                )
        if sizes.rest:
            part = dot(rest_places(sizes, block), values[sizes.tiled_rows :].astype(BF16))
            rest = part if rest is None else rest + part
    if sizes.rest:
        first, each_rest = FEATURE_BLOCKS * tile, FEATURE_BLOCKS * sizes.rest
        for number, piece in enumerate(pieces):
            rows = rest[number * each * each_rest : (number + 1) * each * each_rest]
            piece[:, first:, :] = rows.reshape(each, each_rest, sizes.lanes).astype(BF16)


def write_message(sizes, message, block_values):
    write_pieces(sizes, [message], block_values)


def read_rest(sizes, message):
    if not sizes.rest:
        return None
    first = FEATURE_BLOCKS * sizes.tiled
    return (
        message[:, first:, :]
        .astype(F32)
        .reshape(sizes.rest_rows * FEATURE_BLOCKS, sizes.lanes)
        .astype(BF16)
    )


def read_block(sizes, message, rest, block):
    parts = []
    if sizes.tiled:
        parts.append(
            message[:, block * sizes.tiled : (block + 1) * sizes.tiled, :].reshape(
                sizes.tiled_rows, sizes.lanes
            )
        )
    if sizes.rest:
        parts.append(dot(rest_places_across(sizes, block), rest).astype(BF16))
    return jnp.concatenate(parts, axis=0)


def span(sizes, block):
    return slice(block * sizes.lanes, (block + 1) * sizes.lanes)


def inverse_rms(sizes, read):
    total = jnp.zeros((sizes.rows, 1), F32)
    for block in range(FEATURE_BLOCKS):
        wide = read(block).astype(F32)
        total = total + jnp.sum(wide * wide, axis=1, keepdims=True)
    return lax.rsqrt(total / sizes.features + EPSILON)


def clip_copy(pick, clips, place, done):
    copy = pltpu.make_async_copy(clips.at[pick[0]], place, done)
    copy.start()
    return copy


def first_kernel(sizes, pick, clips, across, message, clip, done):
    clip_copy(pick, clips, clip, done.at[0]).wait()
    send_normed(sizes, clip, across, message)


def cotangent_kernel(sizes, pick, clips, across, *refs):
    planes, (clip, done) = refs[:PLANES], refs[PLANES:]
    clip_copy(pick, clips, clip, done.at[0]).wait()
    send_weighted(sizes, clip, across, planes, pick[1])


def regroup_kernel(sizes, *refs):
    planes, places = refs[:PLANES], refs[PLANES:]
    for number, place in enumerate(places):
        for plane_number, plane in enumerate(planes):
            place[plane_number] = plane[number]


def far_kernel(*refs):
    *places, plane = refs
    for number, place in enumerate(places):
        plane[number] = place[PLANES - 1]


def send_normed(sizes, carried, across, message):
    scale = inverse_rms(sizes, lambda block: carried[:, span(sizes, block)])
    select = slots_by_token(sizes, across[...], False)

    def values(block):
        normed = (carried[:, span(sizes, block)].astype(F32) * scale).astype(BF16)
        return dot(select, normed)

    write_message(sizes, message, values)


def send_weighted(sizes, incoming, across, pieces, base=0):
    high, low = slots_by_token(sizes, across[...], True, base)

    def values(block):
        rows = incoming[:, span(sizes, block)]
        return dot(high, rows) + dot(low, rows)

    write_pieces(sizes, pieces, values)


def middle_kernel(sizes, before, answer, table, across, carried, message):
    high, low = tokens_by_slot(sizes, table[...], True)
    rest = read_rest(sizes, answer)
    for block in range(FEATURE_BLOCKS):
        rows = read_block(sizes, answer, rest, block)
        mixed = before[:, span(sizes, block)].astype(F32) + (dot(high, rows) + dot(low, rows))
        carried[:, span(sizes, block)] = mixed.astype(BF16)
    send_normed(sizes, carried, across, message)


def norm_back(sizes, carried, incoming, answer, table, result, upstream, copies=()):
    select = tokens_by_slot(sizes, table[...], False)
    rest = read_rest(sizes, answer)
    for copy in copies[:1]:
        copy.wait()
    inner = jnp.zeros((sizes.rows, 1), F32)
    squares = jnp.zeros((sizes.rows, 1), F32)
    for block in range(FEATURE_BLOCKS):
        here = span(sizes, block)
        back = dot(select, read_block(sizes, answer, rest, block))
        wide = carried[:, here].astype(F32)
        upstream[:, here] = back
        inner = inner + jnp.sum(wide * back, axis=1, keepdims=True)
        squares = squares + jnp.sum(wide * wide, axis=1, keepdims=True)
    scale = lax.rsqrt(squares / sizes.features + EPSILON)
    pull = scale * scale * scale * (inner / sizes.features)
    for copy in copies[1:]:
        copy.wait()
    for block in range(FEATURE_BLOCKS):
        here = span(sizes, block)
        wide = carried[:, here].astype(F32)
        result[:, here] = (
            incoming[:, here].astype(F32) + (scale * upstream[:, here] - wide * pull)
        ).astype(BF16)


def last_kernel(
    sizes, pick, before, incoming, answer, table, far,
    result, whole, upstream, clip, grad, apart, done,
):
    copies = [
        pltpu.make_async_copy(before, clip, done.at[0]),
        pltpu.make_async_copy(incoming, grad, done.at[1]),
    ]
    for copy in copies:
        copy.start()
    far_copy = pltpu.make_async_copy(far, apart, done.at[2])
    far_copy.start()
    norm_back(sizes, clip, grad, answer, table, result, upstream, copies)
    far_copy.wait()

    @pl.when(pick[0] == 0)
    def _():
        near_first = pltpu.make_async_copy(result, whole.at[0], done.at[2])
        near_first.start()
        near_first.wait()

    @pl.when(pick[0] != 0)
    def _():
        far_first = pltpu.make_async_copy(apart, whole.at[0], done.at[2])
        near_last = pltpu.make_async_copy(grad, whole.at[1], done.at[3])
        far_first.start()
        near_last.start()
        far_first.wait()
        near_last.wait()


def turn_kernel(sizes, carried, incoming, answer, table, across, result, message, upstream):
    norm_back(sizes, carried, incoming, answer, table, result, upstream)
    send_weighted(sizes, result, across, [message])


def through_up(sizes, received, up):
    rest = read_rest(sizes, received)
    hidden = jnp.zeros((sizes.slots, sizes.hidden), F32)
    for block in range(FEATURE_BLOCKS):
        rows = read_block(sizes, received, rest, block)
        hidden = hidden + dot(rows, up[span(sizes, block), :])
    return hidden


def through_down_back(sizes, received, down):
    rest = read_rest(sizes, received)
    back = jnp.zeros((sizes.slots, sizes.hidden), F32)
    for block in range(FEATURE_BLOCKS):
        rows = read_block(sizes, received, rest, block)
        back = back + dot_last(rows, down[:, span(sizes, block)])
    return back


def back_message(sizes, back_hidden, up, message):
    write_message(sizes, message, lambda block: dot_last(back_hidden, up[span(sizes, block), :]))


def forward_kernel(sizes, received, up, down, hidden_out, activated_out, message):
    hidden = through_up(sizes, received, up)
    hidden_out[...] = hidden
    activated = gelu_value(hidden).astype(BF16)
    activated_out[...] = activated
    write_message(sizes, message, lambda block: dot(activated, down[:, span(sizes, block)]))


def hidden_back_kernel(sizes, pick, down, *refs):
    count, last = sizes.in_plane, PLANES - 1
    places, far, (back_out, received, here, done) = refs[:count], refs[count], refs[count + 1 :]
    copies = []
    for number, place in enumerate(places):
        first = number * PLANES
        copies += [
            pltpu.make_async_copy(
                place.at[pl.ds(0, last)], here.at[pl.ds(first, last)], done.at[number]
            ),
            pltpu.make_async_copy(far.at[number], here.at[first + last], done.at[count + number]),
        ]
    for copy in copies:
        copy.start()
    for copy in copies:
        copy.wait()
    for sender in range(sizes.experts):
        partner = pick[1] ^ sender
        received[sender] = here[(partner % count) * PLANES + partner // count]
    back_out[...] = through_down_back(sizes, received, down)


def turn_expert_kernel(sizes, received, back, up, activated_out, message):
    hidden = through_up(sizes, received, up)
    activated_out[...] = gelu_value(hidden).astype(BF16)
    back_hidden = (back[...] * gelu_slope(hidden)).astype(BF16)
    back_message(sizes, back_hidden, up, message)


def backward_kernel(sizes, received, hidden, up, down, message):
    slope = gelu_slope(hidden[...])
    back = through_down_back(sizes, received, down)
    back_message(sizes, (back * slope).astype(BF16), up, message)


def choose(pick, wanted, sources, places, semaphores):
    count = len(places)

    def begin(chosen):
        for number in range(count):
            pltpu.make_async_copy(chosen[number], places[number], semaphores.at[number]).start()

    @pl.when(pick[0] == wanted)
    def _():
        begin(sources[:count])

    @pl.when(pick[0] != wanted)
    def _():
        begin(sources[count:])

    for number in range(count):
        pltpu.make_async_copy(sources[number], places[number], semaphores.at[number]).wait()


def weights_kernel(pick, up, down, up_other, down_other, up_0, down_0, up_1, down_1, done):
    mine, others = (up, down), (up_other, down_other)
    choose(pick, 0, mine + others + others + mine, (up_0, down_0, up_1, down_1), done)


def assemble_kernel(pick, far, mine, whole, done):
    @pl.when(pick[0] == 0)
    def _():
        copy = pltpu.make_async_copy(far, whole.at[1], done.at[0])
        copy.start()
        copy.wait()


def down_grad_kernel(sizes, pick, *refs):
    sources, result, here, done = refs[:8], refs[8], refs[9:13], refs[13]
    choose(pick, 0, sources, here, done)
    near, near_grad, far, far_grad = here
    rest_near, rest_far = read_rest(sizes, near_grad), read_rest(sizes, far_grad)
    over_rows = (((0,), (0,)), ((), ()))
    for block in range(FEATURE_BLOCKS):
        rows_near = read_block(sizes, near_grad, rest_near, block)
        rows_far = read_block(sizes, far_grad, rest_far, block)
        total = lax.dot_general(near[...], rows_near, over_rows, preferred_element_type=F32)
        total = total + lax.dot_general(far[...], rows_far, over_rows, preferred_element_type=F32)
        result[:, span(sizes, block)] = total.astype(BF16)


TOOK = {
    "weights": 7, "send_tokens": 3, "send_cotangent": 4, "expert_forward": 6, "hidden_back": 5,
    "combine_send": 4, "expert_turn": 6, "norm_back_send": 5, "expert_backward": 6,
    "down_grad": 11, "norm_back_last": 6, "assemble": 1, "regroup": 2, "far_plane": 1,
}
FLOPS_PER_MICROSECOND = 1_150_000_000


VMEM = pl.BlockSpec(memory_space=pltpu.VMEM)
SMEM = pl.BlockSpec(memory_space=pltpu.SMEM)
HBM = pl.BlockSpec(memory_space=pltpu.HBM)


def call(
    kernel, name, operands, outs, scratch=(), specs=None, out_specs=None, aliases=None,
    vmem=VMEM_BYTES,
):
    return pl.pallas_call(
        kernel,
        name=name,
        in_specs=specs or [VMEM] * len(operands),
        out_specs=out_specs or [VMEM] * len(outs),
        out_shape=[
            jax.ShapeDtypeStruct(*out) if isinstance(out, tuple) else out for out in outs
        ],
        scratch_shapes=list(scratch),
        input_output_aliases=aliases or {},
        cost_estimate=pl.CostEstimate(
            flops=TOOK[name] * FLOPS_PER_MICROSECOND, transcendentals=0, bytes_accessed=0
        ),
        compiler_params=pltpu.CompilerParams(vmem_limit_bytes=vmem),
    )(*operands)


def exchange(message):
    return lax.all_to_all(message, "expert", split_axis=0, concat_axis=0, tiled=True)


def to_partner(piece, number):
    if number == 0:
        return piece
    count = lax.axis_size("expert")
    return lax.ppermute(piece, "expert", [(source, source ^ number) for source in range(count)])


def shards(tokens, cotangent, expert_ids, gate_prob, up_weight, down_weight):
    core = lax.axis_index("pipe")
    rows, features = tokens.shape[1], tokens.shape[2]
    hidden = up_weight.shape[3]
    sizes = Sizes(lax.axis_size("expert"), rows, features, hidden)
    swap = [(0, 1), (1, 0)]
    pick = jnp.stack([core, lax.axis_index("expert")]).astype(jnp.int32)

    tables = jnp.concatenate([expert_ids[0].astype(F32), gate_prob[0]], axis=-1).swapaxes(1, 2)
    mine = lax.dynamic_index_in_dim(tables, core, 0, keepdims=False)
    theirs = lax.dynamic_index_in_dim(tables, 1 - core, 0, keepdims=False)
    theirs = lax.ppermute(theirs, "pipe", swap)
    across_0 = jnp.where(core == 0, mine, theirs)
    across_1 = jnp.where(core == 0, theirs, mine)
    table_0, table_1 = across_0.T, across_1.T
    up, down, theirs = lax.optimization_barrier((up_weight[0, 0], down_weight[0, 0], theirs))
    up_other = lax.ppermute(up, "pipe", swap)
    down_other = lax.ppermute(down, "pipe", swap)

    upstream_scratch = pltpu.VMEM((rows, features), F32)
    message = (sizes.message, BF16)
    home_rows = ((rows, features), BF16)
    activated = ((sizes.slots, hidden), BF16)
    wide_hidden = ((sizes.slots, hidden), F32)
    rows_scratch = pltpu.VMEM(*home_rows)
    up_shape, down_shape = ((features, hidden), BF16), ((hidden, features), BF16)

    def kernel(body, *more):
        return functools.partial(body, sizes, *more)

    def done(count):
        return pltpu.SemaphoreType.DMA((count,))

    up_0, down_0, up_1, down_1 = call(
        weights_kernel, "weights", [pick, up, down, up_other, down_other],
        [up_shape, down_shape] * 2, [done(4)], [SMEM] + [HBM] * 4, [HBM] * 4,
    )
    out_0, clip = call(
        kernel(first_kernel), "send_tokens", [pick, tokens, across_0], [message, home_rows],
        [done(1)], [SMEM, HBM, VMEM],
    )
    across_1_late, _, _ = lax.optimization_barrier((across_1, out_0, up_1))
    in_0 = exchange(out_0)
    plane = ((sizes.in_plane,) + sizes.message[1:], BF16)
    place = ((PLANES,) + sizes.message[1:], BF16)
    *planes, clip_grad = call(
        kernel(cotangent_kernel), "send_cotangent", [pick, cotangent, across_1_late],
        [plane] * PLANES + [home_rows], [done(1)], [SMEM, HBM, VMEM],
    )
    last = PLANES - 1
    near = [to_partner(planes[number], number * sizes.in_plane) for number in range(last)]
    hidden_0, activated_0, answer_0 = call(
        kernel(forward_kernel), "expert_forward", [in_0, up_0, down_0],
        [wide_hidden, activated, message],
    )
    *near, answer_0 = lax.optimization_barrier((*near, answer_0))
    returned_0 = exchange(answer_0)
    places = call(
        kernel(regroup_kernel), "regroup", near + [planes[last]], [place] * sizes.in_plane
    )
    places = [to_partner(piece, number) for number, piece in enumerate(places)]
    (far,) = call(far_kernel, "far_plane", places, [plane])
    _, returned_0 = lax.optimization_barrier((far, returned_0))
    far = to_partner(far, last * sizes.in_plane)
    carried_1, out_1 = call(
        kernel(middle_kernel), "combine_send", [clip, returned_0, table_0, across_1],
        [home_rows, message],
    )
    far, out_1 = lax.optimization_barrier((far, out_1))
    in_1 = exchange(out_1)
    back_1, grad_in_1 = call(
        kernel(hidden_back_kernel), "hidden_back", [pick, down_1] + places + [far],
        [wide_hidden, message], [pltpu.VMEM(*message), done(2 * sizes.in_plane)],
        [SMEM, VMEM] + [HBM] * (sizes.in_plane + 1),
    )
    activated_1, picks_1 = call(
        kernel(turn_expert_kernel), "expert_turn", [in_1, back_1, up_1], [activated, message]
    )
    back_home_1 = exchange(picks_1)
    grad_1, grad_out_0 = call(
        kernel(turn_kernel), "norm_back_send",
        [carried_1, clip_grad, back_home_1, table_1, across_0],
        [home_rows, message], [upstream_scratch],
    )
    grad_in_0 = exchange(grad_out_0)
    (picks_0,) = call(
        kernel(backward_kernel), "expert_backward", [grad_in_0, hidden_0, up_0, down_0], [message]
    )
    back_home_0 = exchange(picks_0)

    to_first, to_second = [(1, 0)], [(0, 1)]
    operands = []
    for near, way in (
        ([activated_0, grad_in_0], to_first), ([activated_1, grad_in_1], to_second)
    ):
        operands += near + [lax.ppermute(array, "pipe", way) for array in near]
    (down_grad,) = call(
        kernel(down_grad_kernel), "down_grad", [pick] + operands, [((hidden, features), BF16)],
        [pltpu.VMEM(*activated), pltpu.VMEM(*message)] * 2 + [pltpu.SemaphoreType.DMA((4,))],
        [SMEM] + [HBM] * 8,
    )
    far_1 = lax.ppermute(grad_1, "pipe", to_second)
    down_grad, far_1, back_home_0 = lax.optimization_barrier((down_grad, far_1, back_home_0))
    held = (tokens.shape, BF16)
    grad_0, input_grad = call(
        kernel(last_kernel), "norm_back_last", [pick, clip, grad_1, back_home_0, table_0, far_1],
        [home_rows, held], [upstream_scratch] + [rows_scratch] * 3 + [done(4)],
        [SMEM, HBM, HBM, VMEM, VMEM, HBM], [VMEM, HBM], vmem=WHOLE_VMEM_BYTES,
    )
    far_0 = lax.ppermute(grad_0, "pipe", to_first)
    (input_grad,) = call(
        assemble_kernel, "assemble", [pick, far_0, input_grad], [held], [pltpu.SemaphoreType.DMA((1,))],
        [SMEM, HBM, HBM], [HBM], {2: 0},
    )
    return input_grad[None], down_grad[None, None]


def solution(mesh):
    placed = (
        P(None, "expert", None),
        P(None, "expert", None),
        P("pipe", None, "expert", None),
        P("pipe", None, "expert", None),
        P("pipe", "expert", None, None),
        P("pipe", "expert", None, None),
    )
    return jax.shard_map(
        shards,
        mesh=mesh,
        in_specs=placed,
        out_specs=(P("pipe", None, "expert", None), P("pipe", "expert", None, None)),
        check_vma=False,
    )
```

```python
import functools

import jax
import jax.numpy as jnp
from jax import lax
from jax.experimental import pallas as pl
from jax.experimental.pallas import tpu as pltpu
from jax.sharding import PartitionSpec as P

EPSILON = 1e-06
ROOT_HALF = 0.7071067811865476
INV_ROOT_TAU = 0.3989422804014327
BF16 = jnp.bfloat16
F32 = jnp.float32
FEATURE_BLOCKS = 8
PLANES = 4
SLOT_TILE = 16
VMEM_BYTES = 20 * 1024 * 1024
WHOLE_VMEM_BYTES = 60 * 1024 * 1024


class Sizes:
    def __init__(self, experts, rows, features, hidden):
        self.experts, self.rows, self.features, self.hidden = experts, rows, features, hidden
        self.capacity = 5 * rows // (2 * experts)
        self.lanes = features // FEATURE_BLOCKS
        self.tiled = self.capacity // SLOT_TILE * SLOT_TILE
        self.rest = self.capacity - self.tiled
        self.tiled_rows = experts * self.tiled
        self.rest_rows = experts * self.rest
        self.slots = experts * self.capacity
        self.message = (experts, FEATURE_BLOCKS * self.capacity, self.lanes)
        self.in_plane = experts // PLANES


def bring(source, place, done):
    copy = pltpu.make_async_copy(source, place, done)
    copy.start()
    return copy


def iota(shape, axis):
    return lax.broadcasted_iota(jnp.int32, shape, axis)


def dot(left, right):
    return jnp.dot(left, right, preferred_element_type=F32)


def dot_last(left, right):
    return lax.dot_general(left, right, (((1,), (1,)), ((), ())), preferred_element_type=F32)


def gelu_value(values):
    return 0.5 * values * (1.0 + lax.erf(values * ROOT_HALF))


def gelu_slope(values):
    return (
        0.5 * (1.0 + lax.erf(values * ROOT_HALF))
        + values * jnp.exp(-0.5 * values * values) * INV_ROOT_TAU
    )


def halves(values):
    high = values.astype(BF16)
    return high, (values - high.astype(F32)).astype(BF16)


def slot_parts(sizes):
    parts = []
    if sizes.tiled:
        parts.append((sizes.tiled, 0))
    if sizes.rest:
        parts.append((sizes.rest, sizes.tiled))
    return parts


def expansion(sizes, width):
    count = sizes.experts * width
    shape = (count, sizes.experts)
    first = iota(shape, 1) * width
    row = iota(shape, 0)
    return ((row >= first) & (row < first + width)).astype(BF16)


def expansion_across(sizes, width):
    count = sizes.experts * width
    shape = (sizes.experts, count)
    first = iota(shape, 0) * width
    column = iota(shape, 1)
    return ((column >= first) & (column < first + width)).astype(BF16)


def slots_by_token(sizes, table_across, gated, base=0):
    rows = sizes.rows
    names = (iota((sizes.experts, rows), 0) ^ base).astype(F32)
    first = table_across[0:1, :] == names
    second = table_across[1:2, :] == names
    chosen = jnp.where(first | second, 1.0, 0.0)
    earlier = (iota((rows, rows), 0) < iota((rows, rows), 1)).astype(BF16)
    rank = jnp.where(chosen > 0.0, dot(chosen.astype(BF16), earlier), -1.0).astype(BF16)
    if gated:
        gate = jnp.where(first, table_across[2:3, :], 0.0) + jnp.where(
            second, table_across[3:4, :], 0.0
        )
        high, low = halves(gate)
    ones, highs, lows = [], [], []
    for width, start in slot_parts(sizes):
        spread = expansion(sizes, width)
        ranks = dot(spread, rank)
        place = iota(ranks.shape, 0) % width + start
        here = ranks == place.astype(F32)
        if gated:
            highs.append(jnp.where(here, dot(spread, high), 0.0).astype(BF16))
            lows.append(jnp.where(here, dot(spread, low), 0.0).astype(BF16))
        else:
            ones.append(jnp.where(here, 1.0, 0.0).astype(BF16))
    if gated:
        return jnp.concatenate(highs, axis=0), jnp.concatenate(lows, axis=0)
    return jnp.concatenate(ones, axis=0)


def tokens_by_slot(sizes, table, gated):
    rows = sizes.rows
    names = iota((rows, sizes.experts), 1).astype(F32)
    first = table[:, 0:1] == names
    second = table[:, 1:2] == names
    chosen = jnp.where(first | second, 1.0, 0.0)
    earlier = (iota((rows, rows), 1) < iota((rows, rows), 0)).astype(BF16)
    rank = jnp.where(chosen > 0.0, dot(earlier, chosen.astype(BF16)), -1.0).astype(BF16)
    if gated:
        gate = jnp.where(first, table[:, 2:3], 0.0) + jnp.where(second, table[:, 3:4], 0.0)
        high, low = halves(gate)
    ones, highs, lows = [], [], []
    for width, start in slot_parts(sizes):
        spread = expansion_across(sizes, width)
        ranks = dot(rank, spread)
        place = iota(ranks.shape, 1) % width + start
        here = ranks == place.astype(F32)
        if gated:
            highs.append(jnp.where(here, dot(high, spread), 0.0).astype(BF16))
            lows.append(jnp.where(here, dot(low, spread), 0.0).astype(BF16))
        else:
            ones.append(jnp.where(here, 1.0, 0.0).astype(BF16))
    if gated:
        return jnp.concatenate(highs, axis=1), jnp.concatenate(lows, axis=1)
    return jnp.concatenate(ones, axis=1)


def rest_places(sizes, block):
    shape = (sizes.rest_rows * FEATURE_BLOCKS, sizes.rest_rows)
    return (iota(shape, 0) == iota(shape, 1) * FEATURE_BLOCKS + block).astype(BF16)


def rest_places_across(sizes, block):
    shape = (sizes.rest_rows, sizes.rest_rows * FEATURE_BLOCKS)
    return (iota(shape, 1) == iota(shape, 0) * FEATURE_BLOCKS + block).astype(BF16)


def write_pieces(sizes, pieces, block_values):
    tile, each = sizes.tiled, sizes.experts // len(pieces)
    rest = None
    for block in range(FEATURE_BLOCKS):
        values = block_values(block)
        if tile:
            for number, piece in enumerate(pieces):
                rows = values[number * each * tile : (number + 1) * each * tile].astype(BF16)
                piece[:, block * tile : (block + 1) * tile, :] = rows.reshape(
                    each, tile, sizes.lanes
                )
        if sizes.rest:
            part = dot(rest_places(sizes, block), values[sizes.tiled_rows :].astype(BF16))
            rest = part if rest is None else rest + part
    if sizes.rest:
        first, each_rest = FEATURE_BLOCKS * tile, FEATURE_BLOCKS * sizes.rest
        for number, piece in enumerate(pieces):
            rows = rest[number * each * each_rest : (number + 1) * each * each_rest]
            piece[:, first:, :] = rows.reshape(each, each_rest, sizes.lanes).astype(BF16)


def write_message(sizes, message, block_values):
    write_pieces(sizes, [message], block_values)


def read_rest(sizes, message):
    if not sizes.rest:
        return None
    first = FEATURE_BLOCKS * sizes.tiled
    return (
        message[:, first:, :]
        .astype(F32)
        .reshape(sizes.rest_rows * FEATURE_BLOCKS, sizes.lanes)
        .astype(BF16)
    )


def read_block(sizes, message, rest, block):
    parts = []
    if sizes.tiled:
        parts.append(
            message[:, block * sizes.tiled : (block + 1) * sizes.tiled, :].reshape(
                sizes.tiled_rows, sizes.lanes
            )
        )
    if sizes.rest:
        parts.append(dot(rest_places_across(sizes, block), rest).astype(BF16))
    return jnp.concatenate(parts, axis=0)


def span(sizes, block):
    return slice(block * sizes.lanes, (block + 1) * sizes.lanes)


def inverse_rms(sizes, read):
    total = jnp.zeros((sizes.rows, 1), F32)
    for block in range(FEATURE_BLOCKS):
        wide = read(block).astype(F32)
        total = total + jnp.sum(wide * wide, axis=1, keepdims=True)
    return lax.rsqrt(total / sizes.features + EPSILON)


def cotangent_kernel(sizes, pick, clip, across, *planes):
    send_weighted(sizes, clip, across, planes, pick[1])


def regroup_kernel(sizes, *refs):
    planes, places = refs[:PLANES], refs[PLANES:]
    for number, place in enumerate(places):
        for plane_number, plane in enumerate(planes):
            place[plane_number] = plane[number]


def far_kernel(*refs):
    *places, plane = refs
    for number, place in enumerate(places):
        plane[number] = place[PLANES - 1]


def send_normed(sizes, carried, across, message):
    scale = inverse_rms(sizes, lambda block: carried[:, span(sizes, block)])
    select = slots_by_token(sizes, across[...], False)

    def values(block):
        normed = (carried[:, span(sizes, block)].astype(F32) * scale).astype(BF16)
        return dot(select, normed)

    write_message(sizes, message, values)


def send_weighted(sizes, incoming, across, pieces, base=0):
    high, low = slots_by_token(sizes, across[...], True, base)

    def values(block):
        rows = incoming[:, span(sizes, block)]
        return dot(high, rows) + dot(low, rows)

    write_pieces(sizes, pieces, values)


def middle_kernel(sizes, before, answer, table, across, carried, message):
    high, low = tokens_by_slot(sizes, table[...], True)
    rest = read_rest(sizes, answer)
    for block in range(FEATURE_BLOCKS):
        rows = read_block(sizes, answer, rest, block)
        mixed = before[:, span(sizes, block)].astype(F32) + (dot(high, rows) + dot(low, rows))
        carried[:, span(sizes, block)] = mixed.astype(BF16)
    send_normed(sizes, carried, across, message)


def norm_back(sizes, carried, incoming, answer, table, result, upstream, copies=()):
    select = tokens_by_slot(sizes, table[...], False)
    for copy in copies[:2]:
        copy.wait()
    rest = read_rest(sizes, answer)
    inner = jnp.zeros((sizes.rows, 1), F32)
    squares = jnp.zeros((sizes.rows, 1), F32)
    for block in range(FEATURE_BLOCKS):
        here = span(sizes, block)
        back = dot(select, read_block(sizes, answer, rest, block))
        wide = carried[:, here].astype(F32)
        upstream[:, here] = back
        inner = inner + jnp.sum(wide * back, axis=1, keepdims=True)
        squares = squares + jnp.sum(wide * wide, axis=1, keepdims=True)
    scale = lax.rsqrt(squares / sizes.features + EPSILON)
    pull = scale * scale * scale * (inner / sizes.features)
    for copy in copies[2:]:
        copy.wait()
    for block in range(FEATURE_BLOCKS):
        here = span(sizes, block)
        wide = carried[:, here].astype(F32)
        result[:, here] = (
            incoming[:, here].astype(F32) + (scale * upstream[:, here] - wide * pull)
        ).astype(BF16)


def hold_kernel(pick, grad, far, whole, done):
    @pl.when(pick[0] != 0)
    def _():
        copies = [bring(far, whole.at[0], done.at[0]), bring(grad, whole.at[1], done.at[1])]
        for copy in copies:
            copy.wait()


def assemble_kernel(pick, far, held, whole, done):
    @pl.when(pick[0] == 0)
    def _():
        bring(far, whole.at[1], done.at[0]).wait()


def last_kernel(
    sizes, pick, before, incoming, answer_far, table, held, result, whole,
    upstream, clip, grad, answer, done,
):
    copies = [
        bring(answer_far, answer, done.at[0]),
        bring(before, clip, done.at[1]),
        bring(incoming, grad, done.at[2]),
    ]
    norm_back(sizes, clip, grad, answer, table, result, upstream, copies)

    @pl.when(pick[0] == 0)
    def _():
        bring(result, whole.at[0], done.at[3]).wait()


def turn_kernel(sizes, carried, incoming, answer, table, across, result, message, upstream):
    norm_back(sizes, carried, incoming, answer, table, result, upstream)
    send_weighted(sizes, result, across, [message])


def through_up(sizes, received, up):
    rest = read_rest(sizes, received)
    hidden = jnp.zeros((sizes.slots, sizes.hidden), F32)
    for block in range(FEATURE_BLOCKS):
        rows = read_block(sizes, received, rest, block)
        hidden = hidden + dot(rows, up[span(sizes, block), :])
    return hidden


def through_down_back(sizes, received, down):
    rest = read_rest(sizes, received)
    back = jnp.zeros((sizes.slots, sizes.hidden), F32)
    for block in range(FEATURE_BLOCKS):
        rows = read_block(sizes, received, rest, block)
        back = back + dot_last(rows, down[:, span(sizes, block)])
    return back


def back_message(sizes, back_hidden, up, message):
    write_message(sizes, message, lambda block: dot_last(back_hidden, up[span(sizes, block), :]))


def forward_kernel(sizes, received, up, down, hidden_out, activated_out, message):
    hidden = through_up(sizes, received, up)
    hidden_out[...] = hidden
    activated = gelu_value(hidden).astype(BF16)
    activated_out[...] = activated
    write_message(sizes, message, lambda block: dot(activated, down[:, span(sizes, block)]))


def hidden_back_kernel(sizes, pick, down, *refs):
    count, last = sizes.in_plane, PLANES - 1
    places, far, (back_out, received, here, done) = refs[:count], refs[count], refs[count + 1 :]
    copies = []
    for number, place in enumerate(places):
        first = number * PLANES
        copies += [
            pltpu.make_async_copy(
                place.at[pl.ds(0, last)], here.at[pl.ds(first, last)], done.at[number]
            ),
            pltpu.make_async_copy(far.at[number], here.at[first + last], done.at[count + number]),
        ]
    for copy in copies:
        copy.start()
    for copy in copies:
        copy.wait()
    for sender in range(sizes.experts):
        partner = pick[1] ^ sender
        received[sender] = here[(partner % count) * PLANES + partner // count]
    back_out[...] = through_down_back(sizes, received, down)


def turn_expert_kernel(sizes, received, back, up, activated_out, message):
    hidden = through_up(sizes, received, up)
    activated_out[...] = gelu_value(hidden).astype(BF16)
    back_hidden = (back[...] * gelu_slope(hidden)).astype(BF16)
    back_message(sizes, back_hidden, up, message)


def backward_kernel(sizes, received, hidden, up, down, message):
    slope = gelu_slope(hidden[...])
    back = through_down_back(sizes, received, down)
    back_message(sizes, (back * slope).astype(BF16), up, message)


def choose(pick, wanted, sources, places, semaphores):
    count = len(places)

    def begin(chosen):
        for number in range(count):
            pltpu.make_async_copy(chosen[number], places[number], semaphores.at[number]).start()

    @pl.when(pick[0] == wanted)
    def _():
        begin(sources[:count])

    @pl.when(pick[0] != wanted)
    def _():
        begin(sources[count:])

    for number in range(count):
        pltpu.make_async_copy(sources[number], places[number], semaphores.at[number]).wait()


def weights_kernel(pick, up, down, up_other, down_other, up_0, down_0, up_1, down_1, done):
    mine, others = (up, down), (up_other, down_other)
    choose(pick, 0, mine + others + others + mine, (up_0, down_0, up_1, down_1), done)


def down_grad_kernel(sizes, pick, *refs):
    sources, result, here, done = refs[:8], refs[8], refs[9:13], refs[13]
    choose(pick, 0, sources, here, done)
    near, near_grad, far, far_grad = here
    rest_near, rest_far = read_rest(sizes, near_grad), read_rest(sizes, far_grad)
    over_rows = (((0,), (0,)), ((), ()))
    for block in range(FEATURE_BLOCKS):
        rows_near = read_block(sizes, near_grad, rest_near, block)
        rows_far = read_block(sizes, far_grad, rest_far, block)
        total = lax.dot_general(near[...], rows_near, over_rows, preferred_element_type=F32)
        total = total + lax.dot_general(far[...], rows_far, over_rows, preferred_element_type=F32)
        result[:, span(sizes, block)] = total.astype(BF16)


TOOK = {
    "weights": 7, "send_tokens": 3, "send_cotangent": 4, "expert_forward": 6, "hidden_back": 5,
    "combine_send": 4, "expert_turn": 6, "norm_back_send": 5, "expert_backward": 6,
    "down_grad": 11, "norm_back_last": 6, "hold": 1, "assemble": 1, "regroup": 2, "far_plane": 1,
}
FLOPS_PER_MICROSECOND = 1_150_000_000


VMEM = pl.BlockSpec(memory_space=pltpu.VMEM)
SMEM = pl.BlockSpec(memory_space=pltpu.SMEM)
HBM = pl.BlockSpec(memory_space=pltpu.HBM)


def call(
    kernel, name, operands, outs, scratch=(), specs=None, out_specs=None, aliases=None,
    vmem=VMEM_BYTES,
):
    return pl.pallas_call(
        kernel,
        name=name,
        in_specs=specs or [VMEM] * len(operands),
        out_specs=out_specs or [VMEM] * len(outs),
        out_shape=[
            jax.ShapeDtypeStruct(*out) if isinstance(out, tuple) else out for out in outs
        ],
        scratch_shapes=list(scratch),
        input_output_aliases=aliases or {},
        cost_estimate=pl.CostEstimate(
            flops=TOOK[name] * FLOPS_PER_MICROSECOND, transcendentals=0, bytes_accessed=0
        ),
        compiler_params=pltpu.CompilerParams(vmem_limit_bytes=vmem),
    )(*operands)


def exchange(message):
    return lax.all_to_all(message, "expert", split_axis=0, concat_axis=0, tiled=True)


def to_partner(piece, number):
    if number == 0:
        return piece
    count = lax.axis_size("expert")
    return lax.ppermute(piece, "expert", [(source, source ^ number) for source in range(count)])


def shards(tokens, cotangent, expert_ids, gate_prob, up_weight, down_weight):
    core = lax.axis_index("pipe")
    rows, features = tokens.shape[1], tokens.shape[2]
    hidden = up_weight.shape[3]
    sizes = Sizes(lax.axis_size("expert"), rows, features, hidden)
    swap = [(0, 1), (1, 0)]
    pick = jnp.stack([core, lax.axis_index("expert")]).astype(jnp.int32)

    tables = jnp.concatenate([expert_ids[0].astype(F32), gate_prob[0]], axis=-1).swapaxes(1, 2)
    mine = lax.dynamic_index_in_dim(tables, core, 0, keepdims=False)
    theirs = lax.dynamic_index_in_dim(tables, 1 - core, 0, keepdims=False)
    theirs = lax.ppermute(theirs, "pipe", swap)
    clip = lax.dynamic_index_in_dim(tokens, core, 0, keepdims=False)
    clip_grad = lax.dynamic_index_in_dim(cotangent, core, 0, keepdims=False)
    across_0 = jnp.where(core == 0, mine, theirs)
    across_1 = jnp.where(core == 0, theirs, mine)
    table_0, table_1 = across_0.T, across_1.T
    up, down, theirs = lax.optimization_barrier((up_weight[0, 0], down_weight[0, 0], theirs))
    up_other = lax.ppermute(up, "pipe", swap)
    down_other = lax.ppermute(down, "pipe", swap)

    upstream_scratch = pltpu.VMEM((rows, features), F32)
    message = (sizes.message, BF16)
    home_rows = ((rows, features), BF16)
    activated = ((sizes.slots, hidden), BF16)
    wide_hidden = ((sizes.slots, hidden), F32)
    rows_scratch = pltpu.VMEM(*home_rows)
    up_shape, down_shape = ((features, hidden), BF16), ((hidden, features), BF16)

    def kernel(body, *more):
        return functools.partial(body, sizes, *more)

    def done(count):
        return pltpu.SemaphoreType.DMA((count,))

    up_0, down_0, up_1, down_1 = call(
        weights_kernel, "weights", [pick, up, down, up_other, down_other],
        [up_shape, down_shape] * 2, [done(4)], [SMEM] + [HBM] * 4, [HBM] * 4,
    )
    (out_0,) = call(kernel(send_normed), "send_tokens", [clip, across_0], [message])
    across_1_late, _, _ = lax.optimization_barrier((across_1, out_0, up_1))
    in_0 = exchange(out_0)
    plane = ((sizes.in_plane,) + sizes.message[1:], BF16)
    place = ((PLANES,) + sizes.message[1:], BF16)
    planes = call(
        kernel(cotangent_kernel), "send_cotangent", [pick, clip_grad, across_1_late],
        [plane] * PLANES, (), [SMEM, VMEM, VMEM],
    )
    last = PLANES - 1
    near = [to_partner(planes[number], number * sizes.in_plane) for number in range(last)]
    hidden_0, activated_0, answer_0 = call(
        kernel(forward_kernel), "expert_forward", [in_0, up_0, down_0],
        [wide_hidden, activated, message],
    )
    *near, answer_0 = lax.optimization_barrier((*near, answer_0))
    returned_0 = exchange(answer_0)
    places = call(
        kernel(regroup_kernel), "regroup", near + [planes[last]], [place] * sizes.in_plane
    )
    places = [to_partner(piece, number) for number, piece in enumerate(places)]
    (far,) = call(far_kernel, "far_plane", places, [plane])
    _, returned_0 = lax.optimization_barrier((far, returned_0))
    far = to_partner(far, last * sizes.in_plane)
    carried_1, out_1 = call(
        kernel(middle_kernel), "combine_send", [clip, returned_0, table_0, across_1],
        [home_rows, message],
    )
    far, out_1 = lax.optimization_barrier((far, out_1))
    in_1 = exchange(out_1)
    back_1, grad_in_1 = call(
        kernel(hidden_back_kernel), "hidden_back", [pick, down_1] + places + [far],
        [wide_hidden, message], [pltpu.VMEM(*message), done(2 * sizes.in_plane)],
        [SMEM, VMEM] + [HBM] * (sizes.in_plane + 1),
    )
    activated_1, picks_1 = call(
        kernel(turn_expert_kernel), "expert_turn", [in_1, back_1, up_1], [activated, message]
    )
    back_home_1 = exchange(picks_1)
    grad_1, grad_out_0 = call(
        kernel(turn_kernel), "norm_back_send",
        [carried_1, clip_grad, back_home_1, table_1, across_0],
        [home_rows, message], [upstream_scratch],
    )
    grad_in_0 = exchange(grad_out_0)
    (picks_0,) = call(
        kernel(backward_kernel), "expert_backward", [grad_in_0, hidden_0, up_0, down_0], [message]
    )
    back_home_0 = exchange(picks_0)

    to_first, to_second = [(1, 0)], [(0, 1)]
    operands = []
    for near, way in (
        ([activated_0, grad_in_0], to_first), ([activated_1, grad_in_1], to_second)
    ):
        operands += near + [lax.ppermute(array, "pipe", way) for array in near]
    (down_grad,) = call(
        kernel(down_grad_kernel), "down_grad", [pick] + operands, [((hidden, features), BF16)],
        [pltpu.VMEM(*activated), pltpu.VMEM(*message)] * 2 + [pltpu.SemaphoreType.DMA((4,))],
        [SMEM] + [HBM] * 8,
    )
    far_1 = lax.ppermute(grad_1, "pipe", to_second)
    held = (tokens.shape, BF16)
    (input_grad,) = call(
        hold_kernel, "hold", [pick, grad_1, far_1], [held], [done(2)], [SMEM, HBM, HBM], [HBM]
    )
    down_grad, input_grad, back_home_0 = lax.optimization_barrier(
        (down_grad, input_grad, back_home_0)
    )
    grad_0, input_grad = call(
        kernel(last_kernel), "norm_back_last",
        [pick, clip, grad_1, back_home_0, table_0, input_grad], [home_rows, held],
        [upstream_scratch, rows_scratch, rows_scratch, pltpu.VMEM(*message), done(4)],
        [SMEM, HBM, HBM, HBM, VMEM, HBM], [VMEM, HBM], {5: 1}, WHOLE_VMEM_BYTES,
    )
    far_0 = lax.ppermute(grad_0, "pipe", to_first)
    (input_grad,) = call(
        assemble_kernel, "assemble", [pick, far_0, input_grad], [held], [done(1)],
        [SMEM, HBM, HBM], [HBM], {2: 0},
    )
    return input_grad[None], down_grad[None, None]


def solution(mesh):
    placed = (
        P(None, "expert", None),
        P(None, "expert", None),
        P("pipe", None, "expert", None),
        P("pipe", None, "expert", None),
        P("pipe", "expert", None, None),
        P("pipe", "expert", None, None),
    )
    return jax.shard_map(
        shards,
        mesh=mesh,
        in_specs=placed,
        out_specs=(P("pipe", None, "expert", None), P("pipe", "expert", None, None)),
        check_vma=False,
    )
```

```python
import functools

import jax
import jax.numpy as jnp
from jax import lax
from jax.experimental import pallas as pl
from jax.experimental.pallas import tpu as pltpu
from jax.sharding import PartitionSpec as P

EPSILON = 1e-06
ROOT_HALF = 0.7071067811865476
INV_ROOT_TAU = 0.3989422804014327
BF16 = jnp.bfloat16
F32 = jnp.float32
FEATURE_BLOCKS = 8
PLANES = 4
SLOT_TILE = 16
FEW_REST_ROWS = 32
VMEM_BYTES = 20 * 1024 * 1024
WHOLE_VMEM_BYTES = 60 * 1024 * 1024


class Sizes:
    def __init__(self, experts, rows, features, hidden):
        self.experts, self.rows, self.features, self.hidden = experts, rows, features, hidden
        self.capacity = 5 * rows // (2 * experts)
        self.lanes = features // FEATURE_BLOCKS
        self.tiled = self.capacity // SLOT_TILE * SLOT_TILE
        self.rest = self.capacity - self.tiled
        self.tiled_rows = experts * self.tiled
        self.rest_rows = experts * self.rest
        self.slots = experts * self.capacity
        self.message = (experts, FEATURE_BLOCKS * self.capacity, self.lanes)
        self.in_plane = experts // PLANES


def bring(source, place, done):
    copy = pltpu.make_async_copy(source, place, done)
    copy.start()
    return copy


def iota(shape, axis):
    return lax.broadcasted_iota(jnp.int32, shape, axis)


def dot(left, right):
    return jnp.dot(left, right, preferred_element_type=F32)


def dot_last(left, right):
    return lax.dot_general(left, right, (((1,), (1,)), ((), ())), preferred_element_type=F32)


def gelu_value(values):
    return 0.5 * values * (1.0 + lax.erf(values * ROOT_HALF))


def gelu_slope(values):
    return (
        0.5 * (1.0 + lax.erf(values * ROOT_HALF))
        + values * jnp.exp(-0.5 * values * values) * INV_ROOT_TAU
    )


def halves(values):
    high = values.astype(BF16)
    return high, (values - high.astype(F32)).astype(BF16)


def slot_parts(sizes):
    parts = []
    if sizes.tiled:
        parts.append((sizes.tiled, 0))
    if sizes.rest:
        parts.append((sizes.rest, sizes.tiled))
    return parts


def expansion(sizes, width):
    count = sizes.experts * width
    shape = (count, sizes.experts)
    first = iota(shape, 1) * width
    row = iota(shape, 0)
    return ((row >= first) & (row < first + width)).astype(BF16)


def expansion_across(sizes, width):
    count = sizes.experts * width
    shape = (sizes.experts, count)
    first = iota(shape, 0) * width
    column = iota(shape, 1)
    return ((column >= first) & (column < first + width)).astype(BF16)


def slots_by_token(sizes, table_across, gated, base=0):
    rows = sizes.rows
    names = (iota((sizes.experts, rows), 0) ^ base).astype(F32)
    first = table_across[0:1, :] == names
    second = table_across[1:2, :] == names
    chosen = jnp.where(first | second, 1.0, 0.0)
    earlier = (iota((rows, rows), 0) < iota((rows, rows), 1)).astype(BF16)
    rank = jnp.where(chosen > 0.0, dot(chosen.astype(BF16), earlier), -1.0).astype(BF16)
    if gated:
        gate = jnp.where(first, table_across[2:3, :], 0.0) + jnp.where(
            second, table_across[3:4, :], 0.0
        )
        high, low = halves(gate)
    ones, highs, lows = [], [], []
    for width, start in slot_parts(sizes):
        spread = expansion(sizes, width)
        ranks = dot(spread, rank)
        place = iota(ranks.shape, 0) % width + start
        here = ranks == place.astype(F32)
        if gated:
            highs.append(jnp.where(here, dot(spread, high), 0.0).astype(BF16))
            lows.append(jnp.where(here, dot(spread, low), 0.0).astype(BF16))
        else:
            ones.append(jnp.where(here, 1.0, 0.0).astype(BF16))
    if gated:
        return jnp.concatenate(highs, axis=0), jnp.concatenate(lows, axis=0)
    return jnp.concatenate(ones, axis=0)


def tokens_by_slot(sizes, table, gated):
    rows = sizes.rows
    names = iota((rows, sizes.experts), 1).astype(F32)
    first = table[:, 0:1] == names
    second = table[:, 1:2] == names
    chosen = jnp.where(first | second, 1.0, 0.0)
    earlier = (iota((rows, rows), 1) < iota((rows, rows), 0)).astype(BF16)
    rank = jnp.where(chosen > 0.0, dot(earlier, chosen.astype(BF16)), -1.0).astype(BF16)
    if gated:
        gate = jnp.where(first, table[:, 2:3], 0.0) + jnp.where(second, table[:, 3:4], 0.0)
        high, low = halves(gate)
    ones, highs, lows = [], [], []
    for width, start in slot_parts(sizes):
        spread = expansion_across(sizes, width)
        ranks = dot(rank, spread)
        place = iota(ranks.shape, 1) % width + start
        here = ranks == place.astype(F32)
        if gated:
            highs.append(jnp.where(here, dot(high, spread), 0.0).astype(BF16))
            lows.append(jnp.where(here, dot(low, spread), 0.0).astype(BF16))
        else:
            ones.append(jnp.where(here, 1.0, 0.0).astype(BF16))
    if gated:
        return jnp.concatenate(highs, axis=1), jnp.concatenate(lows, axis=1)
    return jnp.concatenate(ones, axis=1)


def rest_places(sizes, block):
    shape = (sizes.rest_rows * FEATURE_BLOCKS, sizes.rest_rows)
    return (iota(shape, 0) == iota(shape, 1) * FEATURE_BLOCKS + block).astype(BF16)


def rest_places_across(sizes, block):
    shape = (sizes.rest_rows, sizes.rest_rows * FEATURE_BLOCKS)
    return (iota(shape, 1) == iota(shape, 0) * FEATURE_BLOCKS + block).astype(BF16)


def all_rest_places(sizes, across):
    rows = sizes.rest_rows
    shape = (rows * FEATURE_BLOCKS, rows * FEATURE_BLOCKS)
    to, source = iota(shape, across), iota(shape, 1 - across)
    return ((to % FEATURE_BLOCKS) * rows + to // FEATURE_BLOCKS == source).astype(BF16)


def few_rest_rows(sizes):
    return sizes.rest_rows <= FEW_REST_ROWS and sizes.rest_rows % SLOT_TILE == 0


def write_pieces(sizes, pieces, block_values):
    tile, each = sizes.tiled, sizes.experts // len(pieces)
    rest, others = None, []
    for block in range(FEATURE_BLOCKS):
        values = block_values(block)
        if tile:
            for number, piece in enumerate(pieces):
                rows = values[number * each * tile : (number + 1) * each * tile].astype(BF16)
                piece[:, block * tile : (block + 1) * tile, :] = rows.reshape(
                    each, tile, sizes.lanes
                )
        if sizes.rest:
            other = values[sizes.tiled_rows :].astype(BF16)
            if few_rest_rows(sizes):
                others.append(other)
            else:
                part = dot(rest_places(sizes, block), other)
                rest = part if rest is None else rest + part
    if others:
        rest = dot(all_rest_places(sizes, 0), jnp.concatenate(others, axis=0))
    if sizes.rest:
        first, each_rest = FEATURE_BLOCKS * tile, FEATURE_BLOCKS * sizes.rest
        for number, piece in enumerate(pieces):
            rows = rest[number * each * each_rest : (number + 1) * each * each_rest]
            piece[:, first:, :] = rows.reshape(each, each_rest, sizes.lanes).astype(BF16)


def write_message(sizes, message, block_values):
    write_pieces(sizes, [message], block_values)


def read_rest(sizes, message):
    if not sizes.rest:
        return None
    first = FEATURE_BLOCKS * sizes.tiled
    rows = message[:, first:, :].astype(F32).reshape(sizes.rest_rows * FEATURE_BLOCKS, sizes.lanes)
    rows = rows.astype(BF16)
    if few_rest_rows(sizes):
        rows = dot(all_rest_places(sizes, 1), rows).astype(BF16)
    return rows


def read_block(sizes, message, rest, block):
    parts = []
    if sizes.tiled:
        parts.append(
            message[:, block * sizes.tiled : (block + 1) * sizes.tiled, :].reshape(
                sizes.tiled_rows, sizes.lanes
            )
        )
    if sizes.rest and few_rest_rows(sizes):
        parts.append(rest[block * sizes.rest_rows : (block + 1) * sizes.rest_rows])
    elif sizes.rest:
        parts.append(dot(rest_places_across(sizes, block), rest).astype(BF16))
    return jnp.concatenate(parts, axis=0)


def span(sizes, block):
    return slice(block * sizes.lanes, (block + 1) * sizes.lanes)


def inverse_rms(sizes, read):
    total = jnp.zeros((sizes.rows, 1), F32)
    for block in range(FEATURE_BLOCKS):
        wide = read(block).astype(F32)
        total = total + jnp.sum(wide * wide, axis=1, keepdims=True)
    return lax.rsqrt(total / sizes.features + EPSILON)


def cotangent_kernel(sizes, pick, clip, across, *planes):
    send_weighted(sizes, clip, across, planes, pick[1])


def regroup_kernel(sizes, *refs):
    planes, places = refs[:PLANES], refs[PLANES:]
    for number, place in enumerate(places):
        for plane_number, plane in enumerate(planes):
            place[plane_number] = plane[number]


def far_kernel(*refs):
    *places, plane = refs
    for number, place in enumerate(places):
        plane[number] = place[PLANES - 1]


def send_normed(sizes, carried, across, message):
    scale = inverse_rms(sizes, lambda block: carried[:, span(sizes, block)])
    select = slots_by_token(sizes, across[...], False)

    def values(block):
        normed = (carried[:, span(sizes, block)].astype(F32) * scale).astype(BF16)
        return dot(select, normed)

    write_message(sizes, message, values)


def send_weighted(sizes, incoming, across, pieces, base=0):
    high, low = slots_by_token(sizes, across[...], True, base)

    def values(block):
        rows = incoming[:, span(sizes, block)]
        return dot(high, rows) + dot(low, rows)

    write_pieces(sizes, pieces, values)


def middle_kernel(sizes, before, answer, table, across, carried, message):
    high, low = tokens_by_slot(sizes, table[...], True)
    rest = read_rest(sizes, answer)
    for block in range(FEATURE_BLOCKS):
        rows = read_block(sizes, answer, rest, block)
        mixed = before[:, span(sizes, block)].astype(F32) + (dot(high, rows) + dot(low, rows))
        carried[:, span(sizes, block)] = mixed.astype(BF16)
    send_normed(sizes, carried, across, message)


def norm_back(sizes, carried, incoming, answer, table, result, upstream, copies=()):
    select = tokens_by_slot(sizes, table[...], False)
    for copy in copies[:2]:
        copy.wait()
    rest = read_rest(sizes, answer)
    inner = jnp.zeros((sizes.rows, 1), F32)
    squares = jnp.zeros((sizes.rows, 1), F32)
    for block in range(FEATURE_BLOCKS):
        here = span(sizes, block)
        back = dot(select, read_block(sizes, answer, rest, block))
        wide = carried[:, here].astype(F32)
        upstream[:, here] = back
        inner = inner + jnp.sum(wide * back, axis=1, keepdims=True)
        squares = squares + jnp.sum(wide * wide, axis=1, keepdims=True)
    scale = lax.rsqrt(squares / sizes.features + EPSILON)
    pull = scale * scale * scale * (inner / sizes.features)
    for copy in copies[2:]:
        copy.wait()
    for block in range(FEATURE_BLOCKS):
        here = span(sizes, block)
        wide = carried[:, here].astype(F32)
        result[:, here] = (
            incoming[:, here].astype(F32) + (scale * upstream[:, here] - wide * pull)
        ).astype(BF16)


def hold_kernel(pick, grad, far, whole, done):
    @pl.when(pick[0] != 0)
    def _():
        copies = [bring(far, whole.at[0], done.at[0]), bring(grad, whole.at[1], done.at[1])]
        for copy in copies:
            copy.wait()


def assemble_kernel(pick, far, held, whole, done):
    @pl.when(pick[0] == 0)
    def _():
        bring(far, whole.at[1], done.at[0]).wait()


def last_kernel(
    sizes, pick, before, incoming, answer_far, table, held, result_out, whole,
    upstream, clip, grad, answer, result, done,
):
    copies = [
        bring(answer_far, answer, done.at[0]),
        bring(before, clip, done.at[1]),
        bring(incoming, grad, done.at[2]),
    ]
    norm_back(sizes, clip, grad, answer, table, result, upstream, copies)

    leaving = bring(result, result_out, done.at[4])

    @pl.when(pick[0] == 0)
    def _():
        bring(result, whole.at[0], done.at[3]).wait()

    leaving.wait()


def turn_kernel(sizes, carried, incoming, answer, table, across, result, message, upstream):
    norm_back(sizes, carried, incoming, answer, table, result, upstream)
    send_weighted(sizes, result, across, [message])


def through_up(sizes, received, up):
    rest = read_rest(sizes, received)
    hidden = jnp.zeros((sizes.slots, sizes.hidden), F32)
    for block in range(FEATURE_BLOCKS):
        rows = read_block(sizes, received, rest, block)
        hidden = hidden + dot(rows, up[span(sizes, block), :])
    return hidden


def through_down_back(sizes, received, down):
    rest = read_rest(sizes, received)
    back = jnp.zeros((sizes.slots, sizes.hidden), F32)
    for block in range(FEATURE_BLOCKS):
        rows = read_block(sizes, received, rest, block)
        back = back + dot_last(rows, down[:, span(sizes, block)])
    return back


def back_message(sizes, back_hidden, up, message):
    write_message(sizes, message, lambda block: dot_last(back_hidden, up[span(sizes, block), :]))


def forward_kernel(sizes, received, up, down, hidden_out, activated_out, message):
    hidden = through_up(sizes, received, up)
    hidden_out[...] = hidden
    activated = gelu_value(hidden).astype(BF16)
    activated_out[...] = activated
    write_message(sizes, message, lambda block: dot(activated, down[:, span(sizes, block)]))


def hidden_back_kernel(sizes, pick, down, *refs):
    count, last = sizes.in_plane, PLANES - 1
    places, far, (back_out, received, here, done) = refs[:count], refs[count], refs[count + 1 :]
    copies = []
    for number, place in enumerate(places):
        first = number * PLANES
        copies += [
            pltpu.make_async_copy(
                place.at[pl.ds(0, last)], here.at[pl.ds(first, last)], done.at[number]
            ),
            pltpu.make_async_copy(far.at[number], here.at[first + last], done.at[count + number]),
        ]
    for copy in copies:
        copy.start()
    for copy in copies:
        copy.wait()
    for sender in range(sizes.experts):
        partner = pick[1] ^ sender
        received[sender] = here[(partner % count) * PLANES + partner // count]
    back_out[...] = through_down_back(sizes, received, down)


def turn_expert_kernel(sizes, received, back, up, activated_out, message):
    hidden = through_up(sizes, received, up)
    activated_out[...] = gelu_value(hidden).astype(BF16)
    back_hidden = (back[...] * gelu_slope(hidden)).astype(BF16)
    back_message(sizes, back_hidden, up, message)


def backward_kernel(sizes, received, hidden, up, down, message):
    slope = gelu_slope(hidden[...])
    back = through_down_back(sizes, received, down)
    back_message(sizes, (back * slope).astype(BF16), up, message)


def choose(pick, wanted, sources, places, semaphores):
    count = len(places)

    def begin(chosen):
        for number in range(count):
            pltpu.make_async_copy(chosen[number], places[number], semaphores.at[number]).start()

    @pl.when(pick[0] == wanted)
    def _():
        begin(sources[:count])

    @pl.when(pick[0] != wanted)
    def _():
        begin(sources[count:])

    for number in range(count):
        pltpu.make_async_copy(sources[number], places[number], semaphores.at[number]).wait()


def weights_kernel(pick, up, down, up_other, down_other, up_0, down_0, up_1, down_1, done):
    mine, others = (up, down), (up_other, down_other)
    choose(pick, 0, mine + others + others + mine, (up_0, down_0, up_1, down_1), done)


def down_grad_kernel(sizes, pick, *refs):
    sources, result, here, done = refs[:8], refs[8], refs[9:13], refs[13]
    choose(pick, 0, sources, here, done)
    near, near_grad, far, far_grad = here
    rest_near, rest_far = read_rest(sizes, near_grad), read_rest(sizes, far_grad)
    over_rows = (((0,), (0,)), ((), ()))
    for block in range(FEATURE_BLOCKS):
        rows_near = read_block(sizes, near_grad, rest_near, block)
        rows_far = read_block(sizes, far_grad, rest_far, block)
        total = lax.dot_general(near[...], rows_near, over_rows, preferred_element_type=F32)
        total = total + lax.dot_general(far[...], rows_far, over_rows, preferred_element_type=F32)
        result[:, span(sizes, block)] = total.astype(BF16)


TOOK = {
    "weights": 7, "send_tokens": 3, "send_cotangent": 4, "expert_forward": 6, "hidden_back": 5,
    "combine_send": 4, "expert_turn": 6, "norm_back_send": 5, "expert_backward": 6,
    "down_grad": 11, "norm_back_last": 6, "hold": 1, "assemble": 1, "regroup": 2, "far_plane": 1,
}
FLOPS_PER_MICROSECOND = 1_150_000_000


VMEM = pl.BlockSpec(memory_space=pltpu.VMEM)
SMEM = pl.BlockSpec(memory_space=pltpu.SMEM)
HBM = pl.BlockSpec(memory_space=pltpu.HBM)


def call(
    kernel, name, operands, outs, scratch=(), specs=None, out_specs=None, aliases=None,
    vmem=VMEM_BYTES,
):
    return pl.pallas_call(
        kernel,
        name=name,
        in_specs=specs or [VMEM] * len(operands),
        out_specs=out_specs or [VMEM] * len(outs),
        out_shape=[
            jax.ShapeDtypeStruct(*out) if isinstance(out, tuple) else out for out in outs
        ],
        scratch_shapes=list(scratch),
        input_output_aliases=aliases or {},
        cost_estimate=pl.CostEstimate(
            flops=TOOK[name] * FLOPS_PER_MICROSECOND, transcendentals=0, bytes_accessed=0
        ),
        compiler_params=pltpu.CompilerParams(vmem_limit_bytes=vmem),
    )(*operands)


def exchange(message):
    return lax.all_to_all(message, "expert", split_axis=0, concat_axis=0, tiled=True)


def to_partner(piece, number):
    if number == 0:
        return piece
    count = lax.axis_size("expert")
    return lax.ppermute(piece, "expert", [(source, source ^ number) for source in range(count)])


def shards(tokens, cotangent, expert_ids, gate_prob, up_weight, down_weight):
    core = lax.axis_index("pipe")
    rows, features = tokens.shape[1], tokens.shape[2]
    hidden = up_weight.shape[3]
    sizes = Sizes(lax.axis_size("expert"), rows, features, hidden)
    swap = [(0, 1), (1, 0)]
    pick = jnp.stack([core, lax.axis_index("expert")]).astype(jnp.int32)

    tables = jnp.concatenate([expert_ids[0].astype(F32), gate_prob[0]], axis=-1).swapaxes(1, 2)
    mine = lax.dynamic_index_in_dim(tables, core, 0, keepdims=False)
    theirs = lax.dynamic_index_in_dim(tables, 1 - core, 0, keepdims=False)
    theirs = lax.ppermute(theirs, "pipe", swap)
    clip = lax.dynamic_index_in_dim(tokens, core, 0, keepdims=False)
    clip_grad = lax.dynamic_index_in_dim(cotangent, core, 0, keepdims=False)
    across_0 = jnp.where(core == 0, mine, theirs)
    across_1 = jnp.where(core == 0, theirs, mine)
    table_0, table_1 = across_0.T, across_1.T
    up, down, theirs = lax.optimization_barrier((up_weight[0, 0], down_weight[0, 0], theirs))
    up_other = lax.ppermute(up, "pipe", swap)
    down_other = lax.ppermute(down, "pipe", swap)

    upstream_scratch = pltpu.VMEM((rows, features), F32)
    message = (sizes.message, BF16)
    home_rows = ((rows, features), BF16)
    activated = ((sizes.slots, hidden), BF16)
    wide_hidden = ((sizes.slots, hidden), F32)
    rows_scratch = pltpu.VMEM(*home_rows)
    up_shape, down_shape = ((features, hidden), BF16), ((hidden, features), BF16)

    def kernel(body, *more):
        return functools.partial(body, sizes, *more)

    def done(count):
        return pltpu.SemaphoreType.DMA((count,))

    up_0, down_0, up_1, down_1 = call(
        weights_kernel, "weights", [pick, up, down, up_other, down_other],
        [up_shape, down_shape] * 2, [done(4)], [SMEM] + [HBM] * 4, [HBM] * 4,
    )
    (out_0,) = call(kernel(send_normed), "send_tokens", [clip, across_0], [message])
    across_1_late, _, _ = lax.optimization_barrier((across_1, out_0, up_1))
    in_0 = exchange(out_0)
    plane = ((sizes.in_plane,) + sizes.message[1:], BF16)
    place = ((PLANES,) + sizes.message[1:], BF16)
    planes = call(
        kernel(cotangent_kernel), "send_cotangent", [pick, clip_grad, across_1_late],
        [plane] * PLANES, (), [SMEM, VMEM, VMEM],
    )
    last = PLANES - 1
    near = [to_partner(planes[number], number * sizes.in_plane) for number in range(last)]
    hidden_0, activated_0, answer_0 = call(
        kernel(forward_kernel), "expert_forward", [in_0, up_0, down_0],
        [wide_hidden, activated, message],
    )
    *near, answer_0 = lax.optimization_barrier((*near, answer_0))
    returned_0 = exchange(answer_0)
    places = call(
        kernel(regroup_kernel), "regroup", near + [planes[last]], [place] * sizes.in_plane
    )
    places = [to_partner(piece, number) for number, piece in enumerate(places)]
    (far,) = call(far_kernel, "far_plane", places, [plane])
    _, returned_0 = lax.optimization_barrier((far, returned_0))
    far = to_partner(far, last * sizes.in_plane)
    carried_1, out_1 = call(
        kernel(middle_kernel), "combine_send", [clip, returned_0, table_0, across_1],
        [home_rows, message],
    )
    far, out_1 = lax.optimization_barrier((far, out_1))
    in_1 = exchange(out_1)
    back_1, grad_in_1 = call(
        kernel(hidden_back_kernel), "hidden_back", [pick, down_1] + places + [far],
        [wide_hidden, message], [pltpu.VMEM(*message), done(2 * sizes.in_plane)],
        [SMEM, VMEM] + [HBM] * (sizes.in_plane + 1),
    )
    activated_1, picks_1 = call(
        kernel(turn_expert_kernel), "expert_turn", [in_1, back_1, up_1], [activated, message]
    )
    back_home_1 = exchange(picks_1)
    grad_1, grad_out_0 = call(
        kernel(turn_kernel), "norm_back_send",
        [carried_1, clip_grad, back_home_1, table_1, across_0],
        [home_rows, message], [upstream_scratch],
    )
    grad_in_0 = exchange(grad_out_0)
    (picks_0,) = call(
        kernel(backward_kernel), "expert_backward", [grad_in_0, hidden_0, up_0, down_0], [message]
    )
    back_home_0 = exchange(picks_0)

    to_first, to_second = [(1, 0)], [(0, 1)]
    operands = []
    for near, way in (
        ([activated_0, grad_in_0], to_first), ([activated_1, grad_in_1], to_second)
    ):
        operands += near + [lax.ppermute(array, "pipe", way) for array in near]
    (down_grad,) = call(
        kernel(down_grad_kernel), "down_grad", [pick] + operands, [((hidden, features), BF16)],
        [pltpu.VMEM(*activated), pltpu.VMEM(*message)] * 2 + [pltpu.SemaphoreType.DMA((4,))],
        [SMEM] + [HBM] * 8,
    )
    far_1 = lax.ppermute(grad_1, "pipe", to_second)
    held = (tokens.shape, BF16)
    (input_grad,) = call(
        hold_kernel, "hold", [pick, grad_1, far_1], [held], [done(2)], [SMEM, HBM, HBM], [HBM]
    )
    down_grad, input_grad, back_home_0 = lax.optimization_barrier(
        (down_grad, input_grad, back_home_0)
    )
    grad_0, input_grad = call(
        kernel(last_kernel), "norm_back_last",
        [pick, clip, grad_1, back_home_0, table_0, input_grad], [home_rows, held],
        [upstream_scratch, rows_scratch, rows_scratch, pltpu.VMEM(*message), rows_scratch, done(5)],
        [SMEM, HBM, HBM, HBM, VMEM, HBM], [HBM, HBM], {5: 1}, WHOLE_VMEM_BYTES,
    )
    far_0 = lax.ppermute(grad_0, "pipe", to_first)
    (input_grad,) = call(
        assemble_kernel, "assemble", [pick, far_0, input_grad], [held], [done(1)],
        [SMEM, HBM, HBM], [HBM], {2: 0},
    )
    return input_grad[None], down_grad[None, None]


def solution(mesh):
    placed = (
        P(None, "expert", None),
        P(None, "expert", None),
        P("pipe", None, "expert", None),
        P("pipe", None, "expert", None),
        P("pipe", "expert", None, None),
        P("pipe", "expert", None, None),
    )
    return jax.shard_map(
        shards,
        mesh=mesh,
        in_specs=placed,
        out_specs=(P("pipe", None, "expert", None), P("pipe", "expert", None, None)),
        check_vma=False,
    )
```

```python
import functools

import jax
import jax.numpy as jnp
from jax import lax
from jax.experimental import pallas as pl
from jax.experimental.pallas import tpu as pltpu
from jax.sharding import PartitionSpec as P

EPSILON = 1e-06
ROOT_HALF = 0.7071067811865476
INV_ROOT_TAU = 0.3989422804014327
BF16 = jnp.bfloat16
F32 = jnp.float32
FEATURE_BLOCKS = 8
PLANES = 4
SLOT_TILE = 16
FEW_REST_ROWS = 32
VMEM_BYTES = 20 * 1024 * 1024
WHOLE_VMEM_BYTES = 60 * 1024 * 1024


class Sizes:
    def __init__(self, experts, rows, features, hidden):
        self.experts, self.rows, self.features, self.hidden = experts, rows, features, hidden
        self.capacity = 5 * rows // (2 * experts)
        self.lanes = features // FEATURE_BLOCKS
        self.tiled = self.capacity // SLOT_TILE * SLOT_TILE
        self.rest = self.capacity - self.tiled
        self.tiled_rows = experts * self.tiled
        self.rest_rows = experts * self.rest
        self.slots = experts * self.capacity
        self.message = (experts, FEATURE_BLOCKS * self.capacity, self.lanes)
        self.in_plane = experts // PLANES


def bring(source, place, done):
    copy = pltpu.make_async_copy(source, place, done)
    copy.start()
    return copy


def iota(shape, axis):
    return lax.broadcasted_iota(jnp.int32, shape, axis)


def dot(left, right):
    return jnp.dot(left, right, preferred_element_type=F32)


def dot_last(left, right):
    return lax.dot_general(left, right, (((1,), (1,)), ((), ())), preferred_element_type=F32)


def gelu_value(values):
    return 0.5 * values * (1.0 + lax.erf(values * ROOT_HALF))


def gelu_slope(values):
    return (
        0.5 * (1.0 + lax.erf(values * ROOT_HALF))
        + values * jnp.exp(-0.5 * values * values) * INV_ROOT_TAU
    )


def halves(values):
    high = values.astype(BF16)
    return high, (values - high.astype(F32)).astype(BF16)


def slot_parts(sizes):
    parts = []
    if sizes.tiled:
        parts.append((sizes.tiled, 0))
    if sizes.rest:
        parts.append((sizes.rest, sizes.tiled))
    return parts


def expansion(sizes, width):
    count = sizes.experts * width
    shape = (count, sizes.experts)
    first = iota(shape, 1) * width
    row = iota(shape, 0)
    return ((row >= first) & (row < first + width)).astype(BF16)


def expansion_across(sizes, width):
    count = sizes.experts * width
    shape = (sizes.experts, count)
    first = iota(shape, 0) * width
    column = iota(shape, 1)
    return ((column >= first) & (column < first + width)).astype(BF16)


def slots_by_token(sizes, table_across, gated, base=0):
    rows = sizes.rows
    names = (iota((sizes.experts, rows), 0) ^ base).astype(F32)
    first = table_across[0:1, :] == names
    second = table_across[1:2, :] == names
    chosen = jnp.where(first | second, 1.0, 0.0)
    earlier = (iota((rows, rows), 0) < iota((rows, rows), 1)).astype(BF16)
    rank = jnp.where(chosen > 0.0, dot(chosen.astype(BF16), earlier), -1.0).astype(BF16)
    if gated:
        gate = jnp.where(first, table_across[2:3, :], 0.0) + jnp.where(
            second, table_across[3:4, :], 0.0
        )
        high, low = halves(gate)
    ones, highs, lows = [], [], []
    for width, start in slot_parts(sizes):
        spread = expansion(sizes, width)
        ranks = dot(spread, rank)
        place = iota(ranks.shape, 0) % width + start
        here = ranks == place.astype(F32)
        if gated:
            highs.append(jnp.where(here, dot(spread, high), 0.0).astype(BF16))
            lows.append(jnp.where(here, dot(spread, low), 0.0).astype(BF16))
        else:
            ones.append(jnp.where(here, 1.0, 0.0).astype(BF16))
    if gated:
        return jnp.concatenate(highs, axis=0), jnp.concatenate(lows, axis=0)
    return jnp.concatenate(ones, axis=0)


def tokens_by_slot(sizes, table, gated):
    rows = sizes.rows
    names = iota((rows, sizes.experts), 1).astype(F32)
    first = table[:, 0:1] == names
    second = table[:, 1:2] == names
    chosen = jnp.where(first | second, 1.0, 0.0)
    earlier = (iota((rows, rows), 1) < iota((rows, rows), 0)).astype(BF16)
    rank = jnp.where(chosen > 0.0, dot(earlier, chosen.astype(BF16)), -1.0).astype(BF16)
    if gated:
        gate = jnp.where(first, table[:, 2:3], 0.0) + jnp.where(second, table[:, 3:4], 0.0)
        high, low = halves(gate)
    ones, highs, lows = [], [], []
    for width, start in slot_parts(sizes):
        spread = expansion_across(sizes, width)
        ranks = dot(rank, spread)
        place = iota(ranks.shape, 1) % width + start
        here = ranks == place.astype(F32)
        if gated:
            highs.append(jnp.where(here, dot(high, spread), 0.0).astype(BF16))
            lows.append(jnp.where(here, dot(low, spread), 0.0).astype(BF16))
        else:
            ones.append(jnp.where(here, 1.0, 0.0).astype(BF16))
    if gated:
        return jnp.concatenate(highs, axis=1), jnp.concatenate(lows, axis=1)
    return jnp.concatenate(ones, axis=1)


def rest_places(sizes, block):
    shape = (sizes.rest_rows * FEATURE_BLOCKS, sizes.rest_rows)
    return (iota(shape, 0) == iota(shape, 1) * FEATURE_BLOCKS + block).astype(BF16)


def rest_places_across(sizes, block):
    shape = (sizes.rest_rows, sizes.rest_rows * FEATURE_BLOCKS)
    return (iota(shape, 1) == iota(shape, 0) * FEATURE_BLOCKS + block).astype(BF16)


def all_rest_places(sizes, across):
    rows = sizes.rest_rows
    shape = (rows * FEATURE_BLOCKS, rows * FEATURE_BLOCKS)
    to, source = iota(shape, across), iota(shape, 1 - across)
    return ((to % FEATURE_BLOCKS) * rows + to // FEATURE_BLOCKS == source).astype(BF16)


def few_rest_rows(sizes):
    return sizes.rest_rows <= FEW_REST_ROWS and sizes.rest_rows % SLOT_TILE == 0


def write_pieces(sizes, pieces, block_values):
    tile, each = sizes.tiled, sizes.experts // len(pieces)
    rest, others = None, []
    for block in range(FEATURE_BLOCKS):
        values = block_values(block)
        if tile:
            for number, piece in enumerate(pieces):
                rows = values[number * each * tile : (number + 1) * each * tile].astype(BF16)
                piece[:, block * tile : (block + 1) * tile, :] = rows.reshape(
                    each, tile, sizes.lanes
                )
        if sizes.rest:
            other = values[sizes.tiled_rows :].astype(BF16)
            if few_rest_rows(sizes):
                others.append(other)
            else:
                part = dot(rest_places(sizes, block), other)
                rest = part if rest is None else rest + part
    if others:
        rest = dot(all_rest_places(sizes, 0), jnp.concatenate(others, axis=0))
    if sizes.rest:
        first, each_rest = FEATURE_BLOCKS * tile, FEATURE_BLOCKS * sizes.rest
        for number, piece in enumerate(pieces):
            rows = rest[number * each * each_rest : (number + 1) * each * each_rest]
            piece[:, first:, :] = rows.reshape(each, each_rest, sizes.lanes).astype(BF16)


def write_message(sizes, message, block_values):
    write_pieces(sizes, [message], block_values)


def read_rest(sizes, message):
    if not sizes.rest:
        return None
    first = FEATURE_BLOCKS * sizes.tiled
    rows = message[:, first:, :].astype(F32).reshape(sizes.rest_rows * FEATURE_BLOCKS, sizes.lanes)
    rows = rows.astype(BF16)
    if few_rest_rows(sizes):
        rows = dot(all_rest_places(sizes, 1), rows).astype(BF16)
    return rows


def read_block(sizes, message, rest, block):
    parts = []
    if sizes.tiled:
        parts.append(
            message[:, block * sizes.tiled : (block + 1) * sizes.tiled, :].reshape(
                sizes.tiled_rows, sizes.lanes
            )
        )
    if sizes.rest and few_rest_rows(sizes):
        parts.append(rest[block * sizes.rest_rows : (block + 1) * sizes.rest_rows])
    elif sizes.rest:
        parts.append(dot(rest_places_across(sizes, block), rest).astype(BF16))
    return jnp.concatenate(parts, axis=0)


def span(sizes, block):
    return slice(block * sizes.lanes, (block + 1) * sizes.lanes)


def inverse_rms(sizes, read):
    total = jnp.zeros((sizes.rows, 1), F32)
    for block in range(FEATURE_BLOCKS):
        wide = read(block).astype(F32)
        total = total + jnp.sum(wide * wide, axis=1, keepdims=True)
    return lax.rsqrt(total / sizes.features + EPSILON)


def cotangent_kernel(sizes, pick, clip, across, *planes):
    send_weighted(sizes, clip, across, planes, pick[1])


def regroup_kernel(sizes, *refs):
    planes, places = refs[:PLANES], refs[PLANES:]
    for number, place in enumerate(places):
        for plane_number, plane in enumerate(planes):
            place[plane_number] = plane[number]


def far_kernel(*refs):
    *places, plane = refs
    for number, place in enumerate(places):
        plane[number] = place[PLANES - 1]


def send_normed(sizes, carried, across, message):
    scale = inverse_rms(sizes, lambda block: carried[:, span(sizes, block)])
    select = slots_by_token(sizes, across[...], False)

    def values(block):
        normed = (carried[:, span(sizes, block)].astype(F32) * scale).astype(BF16)
        return dot(select, normed)

    write_message(sizes, message, values)


def send_weighted(sizes, incoming, across, pieces, base=0):
    high, low = slots_by_token(sizes, across[...], True, base)

    def values(block):
        rows = incoming[:, span(sizes, block)]
        return dot(high, rows) + dot(low, rows)

    write_pieces(sizes, pieces, values)


def middle_kernel(sizes, before, answer, table, across, carried, message):
    high, low = tokens_by_slot(sizes, table[...], True)
    rest = read_rest(sizes, answer)
    for block in range(FEATURE_BLOCKS):
        rows = read_block(sizes, answer, rest, block)
        mixed = before[:, span(sizes, block)].astype(F32) + (dot(high, rows) + dot(low, rows))
        carried[:, span(sizes, block)] = mixed.astype(BF16)
    send_normed(sizes, carried, across, message)


def norm_back(sizes, carried, incoming, answer, table, result, upstream, copies=()):
    select = tokens_by_slot(sizes, table[...], False)
    for copy in copies[:2]:
        copy.wait()
    rest = read_rest(sizes, answer)
    inner = jnp.zeros((sizes.rows, 1), F32)
    squares = jnp.zeros((sizes.rows, 1), F32)
    for block in range(FEATURE_BLOCKS):
        here = span(sizes, block)
        back = dot(select, read_block(sizes, answer, rest, block))
        wide = carried[:, here].astype(F32)
        upstream[:, here] = back
        inner = inner + jnp.sum(wide * back, axis=1, keepdims=True)
        squares = squares + jnp.sum(wide * wide, axis=1, keepdims=True)
    scale = lax.rsqrt(squares / sizes.features + EPSILON)
    pull = scale * scale * scale * (inner / sizes.features)
    for copy in copies[2:]:
        copy.wait()
    for block in range(FEATURE_BLOCKS):
        here = span(sizes, block)
        wide = carried[:, here].astype(F32)
        result[:, here] = (
            incoming[:, here].astype(F32) + (scale * upstream[:, here] - wide * pull)
        ).astype(BF16)


def hold_kernel(pick, grad, far, whole, done):
    @pl.when(pick[0] != 0)
    def _():
        copies = [bring(far, whole.at[0], done.at[0]), bring(grad, whole.at[1], done.at[1])]
        for copy in copies:
            copy.wait()


def assemble_kernel(pick, far, held, whole, done):
    @pl.when(pick[0] == 0)
    def _():
        bring(far, whole.at[1], done.at[0]).wait()


def last_kernel(
    sizes, pick, before, incoming, answer_far, table, held, result_out, whole,
    upstream, clip, grad, answer, result, done,
):
    copies = [
        bring(answer_far, answer, done.at[0]),
        bring(before, clip, done.at[1]),
        bring(incoming, grad, done.at[2]),
    ]
    norm_back(sizes, clip, grad, answer, table, result, upstream, copies)

    leaving = bring(result, result_out, done.at[4])

    @pl.when(pick[0] == 0)
    def _():
        bring(result, whole.at[0], done.at[3]).wait()

    leaving.wait()


def turn_kernel(sizes, carried, incoming, answer, table, across, result, message, upstream):
    norm_back(sizes, carried, incoming, answer, table, result, upstream)
    send_weighted(sizes, result, across, [message])


def through_up(sizes, received, up):
    rest = read_rest(sizes, received)
    hidden = jnp.zeros((sizes.slots, sizes.hidden), F32)
    for block in range(FEATURE_BLOCKS):
        rows = read_block(sizes, received, rest, block)
        hidden = hidden + dot(rows, up[span(sizes, block), :])
    return hidden


def through_down_back(sizes, received, down):
    rest = read_rest(sizes, received)
    back = jnp.zeros((sizes.slots, sizes.hidden), F32)
    for block in range(FEATURE_BLOCKS):
        rows = read_block(sizes, received, rest, block)
        back = back + dot_last(rows, down[:, span(sizes, block)])
    return back


def back_message(sizes, back_hidden, up, message):
    write_message(sizes, message, lambda block: dot_last(back_hidden, up[span(sizes, block), :]))


def forward_kernel(sizes, received, up, down, hidden_out, activated_out, message):
    hidden = through_up(sizes, received, up)
    hidden_out[...] = hidden
    activated = gelu_value(hidden).astype(BF16)
    activated_out[...] = activated
    write_message(sizes, message, lambda block: dot(activated, down[:, span(sizes, block)]))


def hidden_back_kernel(sizes, pick, down, *refs):
    count, last = sizes.in_plane, PLANES - 1
    places, far, (back_out, received, here, done) = refs[:count], refs[count], refs[count + 1 :]
    copies = []
    for number, place in enumerate(places):
        first = number * PLANES
        copies += [
            pltpu.make_async_copy(
                place.at[pl.ds(0, last)], here.at[pl.ds(first, last)], done.at[number]
            ),
            pltpu.make_async_copy(far.at[number], here.at[first + last], done.at[count + number]),
        ]
    for copy in copies:
        copy.start()
    for copy in copies:
        copy.wait()
    for sender in range(sizes.experts):
        partner = pick[1] ^ sender
        plane = partner // count
        received[sender] = here[(partner % count) * PLANES + (plane ^ plane // 2)]
    back_out[...] = through_down_back(sizes, received, down)


def turn_expert_kernel(sizes, received, back, up, activated_out, message):
    hidden = through_up(sizes, received, up)
    activated_out[...] = gelu_value(hidden).astype(BF16)
    back_hidden = (back[...] * gelu_slope(hidden)).astype(BF16)
    back_message(sizes, back_hidden, up, message)


def backward_kernel(sizes, received, hidden, up, down, message):
    slope = gelu_slope(hidden[...])
    back = through_down_back(sizes, received, down)
    back_message(sizes, (back * slope).astype(BF16), up, message)


def choose(pick, wanted, sources, places, semaphores):
    count = len(places)

    def begin(chosen):
        for number in range(count):
            pltpu.make_async_copy(chosen[number], places[number], semaphores.at[number]).start()

    @pl.when(pick[0] == wanted)
    def _():
        begin(sources[:count])

    @pl.when(pick[0] != wanted)
    def _():
        begin(sources[count:])

    for number in range(count):
        pltpu.make_async_copy(sources[number], places[number], semaphores.at[number]).wait()


def weights_kernel(pick, up, down, up_other, down_other, up_0, down_0, up_1, down_1, done):
    mine, others = (up, down), (up_other, down_other)
    choose(pick, 0, mine + others + others + mine, (up_0, down_0, up_1, down_1), done)


def down_grad_kernel(sizes, pick, *refs):
    sources, result, here, done = refs[:8], refs[8], refs[9:13], refs[13]
    choose(pick, 0, sources, here, done)
    near, near_grad, far, far_grad = here
    rest_near, rest_far = read_rest(sizes, near_grad), read_rest(sizes, far_grad)
    over_rows = (((0,), (0,)), ((), ()))
    for block in range(FEATURE_BLOCKS):
        rows_near = read_block(sizes, near_grad, rest_near, block)
        rows_far = read_block(sizes, far_grad, rest_far, block)
        total = lax.dot_general(near[...], rows_near, over_rows, preferred_element_type=F32)
        total = total + lax.dot_general(far[...], rows_far, over_rows, preferred_element_type=F32)
        result[:, span(sizes, block)] = total.astype(BF16)


TOOK = {
    "weights": 7, "send_tokens": 3, "send_cotangent": 4, "expert_forward": 6, "hidden_back": 5,
    "combine_send": 4, "expert_turn": 6, "norm_back_send": 5, "expert_backward": 6,
    "down_grad": 11, "norm_back_last": 6, "hold": 1, "assemble": 1, "regroup": 2, "far_plane": 1,
}
FLOPS_PER_MICROSECOND = 1_150_000_000


VMEM = pl.BlockSpec(memory_space=pltpu.VMEM)
SMEM = pl.BlockSpec(memory_space=pltpu.SMEM)
HBM = pl.BlockSpec(memory_space=pltpu.HBM)


def call(
    kernel, name, operands, outs, scratch=(), specs=None, out_specs=None, aliases=None,
    vmem=VMEM_BYTES,
):
    return pl.pallas_call(
        kernel,
        name=name,
        in_specs=specs or [VMEM] * len(operands),
        out_specs=out_specs or [VMEM] * len(outs),
        out_shape=[
            jax.ShapeDtypeStruct(*out) if isinstance(out, tuple) else out for out in outs
        ],
        scratch_shapes=list(scratch),
        input_output_aliases=aliases or {},
        cost_estimate=pl.CostEstimate(
            flops=TOOK[name] * FLOPS_PER_MICROSECOND, transcendentals=0, bytes_accessed=0
        ),
        compiler_params=pltpu.CompilerParams(vmem_limit_bytes=vmem),
    )(*operands)


def exchange(message):
    return lax.all_to_all(message, "expert", split_axis=0, concat_axis=0, tiled=True)


def to_partner(piece, number):
    if number == 0:
        return piece
    count = lax.axis_size("expert")
    return lax.ppermute(piece, "expert", [(source, source ^ number) for source in range(count)])


def shards(tokens, cotangent, expert_ids, gate_prob, up_weight, down_weight):
    core = lax.axis_index("pipe")
    rows, features = tokens.shape[1], tokens.shape[2]
    hidden = up_weight.shape[3]
    sizes = Sizes(lax.axis_size("expert"), rows, features, hidden)
    swap = [(0, 1), (1, 0)]
    pick = jnp.stack([core, lax.axis_index("expert")]).astype(jnp.int32)

    tables = jnp.concatenate([expert_ids[0].astype(F32), gate_prob[0]], axis=-1).swapaxes(1, 2)
    mine = lax.dynamic_index_in_dim(tables, core, 0, keepdims=False)
    theirs = lax.dynamic_index_in_dim(tables, 1 - core, 0, keepdims=False)
    theirs = lax.ppermute(theirs, "pipe", swap)
    clip = lax.dynamic_index_in_dim(tokens, core, 0, keepdims=False)
    clip_grad = lax.dynamic_index_in_dim(cotangent, core, 0, keepdims=False)
    across_0 = jnp.where(core == 0, mine, theirs)
    across_1 = jnp.where(core == 0, theirs, mine)
    table_0, table_1 = across_0.T, across_1.T
    up, down, theirs = lax.optimization_barrier((up_weight[0, 0], down_weight[0, 0], theirs))
    up_other = lax.ppermute(up, "pipe", swap)
    down_other = lax.ppermute(down, "pipe", swap)

    upstream_scratch = pltpu.VMEM((rows, features), F32)
    message = (sizes.message, BF16)
    home_rows = ((rows, features), BF16)
    activated = ((sizes.slots, hidden), BF16)
    wide_hidden = ((sizes.slots, hidden), F32)
    rows_scratch = pltpu.VMEM(*home_rows)
    up_shape, down_shape = ((features, hidden), BF16), ((hidden, features), BF16)

    def kernel(body, *more):
        return functools.partial(body, sizes, *more)

    def done(count):
        return pltpu.SemaphoreType.DMA((count,))

    up_0, down_0, up_1, down_1 = call(
        weights_kernel, "weights", [pick, up, down, up_other, down_other],
        [up_shape, down_shape] * 2, [done(4)], [SMEM] + [HBM] * 4, [HBM] * 4,
    )
    (out_0,) = call(kernel(send_normed), "send_tokens", [clip, across_0], [message])
    across_1_late, _, _ = lax.optimization_barrier((across_1, out_0, up_1))
    in_0 = exchange(out_0)
    plane = ((sizes.in_plane,) + sizes.message[1:], BF16)
    place = ((PLANES,) + sizes.message[1:], BF16)
    planes = call(
        kernel(cotangent_kernel), "send_cotangent", [pick, clip_grad, across_1_late],
        [plane] * PLANES, (), [SMEM, VMEM, VMEM],
    )
    last = PLANES - 1
    planes = [planes[number ^ number // 2] for number in range(PLANES)]
    near = [
        to_partner(planes[number], (number ^ number // 2) * sizes.in_plane)
        for number in range(last)
    ]
    hidden_0, activated_0, answer_0 = call(
        kernel(forward_kernel), "expert_forward", [in_0, up_0, down_0],
        [wide_hidden, activated, message],
    )
    *near, answer_0 = lax.optimization_barrier((*near, answer_0))
    returned_0 = exchange(answer_0)
    places = call(
        kernel(regroup_kernel), "regroup", near + [planes[last]], [place] * sizes.in_plane
    )
    places = [to_partner(piece, number) for number, piece in enumerate(places)]
    (far,) = call(far_kernel, "far_plane", places, [plane])
    _, returned_0 = lax.optimization_barrier((far, returned_0))
    far = to_partner(far, (last ^ last // 2) * sizes.in_plane)
    carried_1, out_1 = call(
        kernel(middle_kernel), "combine_send", [clip, returned_0, table_0, across_1],
        [home_rows, message],
    )
    far, out_1 = lax.optimization_barrier((far, out_1))
    in_1 = exchange(out_1)
    back_1, grad_in_1 = call(
        kernel(hidden_back_kernel), "hidden_back", [pick, down_1] + places + [far],
        [wide_hidden, message], [pltpu.VMEM(*message), done(2 * sizes.in_plane)],
        [SMEM, VMEM] + [HBM] * (sizes.in_plane + 1),
    )
    activated_1, picks_1 = call(
        kernel(turn_expert_kernel), "expert_turn", [in_1, back_1, up_1], [activated, message]
    )
    back_home_1 = exchange(picks_1)
    grad_1, grad_out_0 = call(
        kernel(turn_kernel), "norm_back_send",
        [carried_1, clip_grad, back_home_1, table_1, across_0],
        [home_rows, message], [upstream_scratch],
    )
    grad_in_0 = exchange(grad_out_0)
    (picks_0,) = call(
        kernel(backward_kernel), "expert_backward", [grad_in_0, hidden_0, up_0, down_0], [message]
    )
    back_home_0 = exchange(picks_0)

    to_first, to_second = [(1, 0)], [(0, 1)]
    operands = []
    for near, way in (
        ([activated_0, grad_in_0], to_first), ([activated_1, grad_in_1], to_second)
    ):
        operands += near + [lax.ppermute(array, "pipe", way) for array in near]
    (down_grad,) = call(
        kernel(down_grad_kernel), "down_grad", [pick] + operands, [((hidden, features), BF16)],
        [pltpu.VMEM(*activated), pltpu.VMEM(*message)] * 2 + [pltpu.SemaphoreType.DMA((4,))],
        [SMEM] + [HBM] * 8,
    )
    far_1 = lax.ppermute(grad_1, "pipe", to_second)
    held = (tokens.shape, BF16)
    (input_grad,) = call(
        hold_kernel, "hold", [pick, grad_1, far_1], [held], [done(2)], [SMEM, HBM, HBM], [HBM]
    )
    down_grad, input_grad, back_home_0 = lax.optimization_barrier(
        (down_grad, input_grad, back_home_0)
    )
    grad_0, input_grad = call(
        kernel(last_kernel), "norm_back_last",
        [pick, clip, grad_1, back_home_0, table_0, input_grad], [home_rows, held],
        [upstream_scratch, rows_scratch, rows_scratch, pltpu.VMEM(*message), rows_scratch, done(5)],
        [SMEM, HBM, HBM, HBM, VMEM, HBM], [HBM, HBM], {5: 1}, WHOLE_VMEM_BYTES,
    )
    far_0 = lax.ppermute(grad_0, "pipe", to_first)
    (input_grad,) = call(
        assemble_kernel, "assemble", [pick, far_0, input_grad], [held], [done(1)],
        [SMEM, HBM, HBM], [HBM], {2: 0},
    )
    return input_grad[None], down_grad[None, None]


def solution(mesh):
    placed = (
        P(None, "expert", None),
        P(None, "expert", None),
        P("pipe", None, "expert", None),
        P("pipe", None, "expert", None),
        P("pipe", "expert", None, None),
        P("pipe", "expert", None, None),
    )
    return jax.shard_map(
        shards,
        mesh=mesh,
        in_specs=placed,
        out_specs=(P("pipe", None, "expert", None), P("pipe", "expert", None, None)),
        check_vma=False,
    )
```

```python
import functools

import jax
import jax.numpy as jnp
from jax import lax
from jax.experimental import pallas as pl
from jax.experimental.pallas import tpu as pltpu
from jax.sharding import PartitionSpec as P

EPSILON = 1e-06
ROOT_HALF = 0.7071067811865476
INV_ROOT_TAU = 0.3989422804014327
BF16 = jnp.bfloat16
F32 = jnp.float32
FEATURE_BLOCKS = 8
PLANES = 4
SLOT_TILE = 16
FEW_REST_ROWS = 32
VMEM_BYTES = 20 * 1024 * 1024
WHOLE_VMEM_BYTES = 60 * 1024 * 1024


class Sizes:
    def __init__(self, experts, rows, features, hidden):
        self.experts, self.rows, self.features, self.hidden = experts, rows, features, hidden
        self.capacity = 5 * rows // (2 * experts)
        self.lanes = features // FEATURE_BLOCKS
        self.tiled = self.capacity // SLOT_TILE * SLOT_TILE
        self.rest = self.capacity - self.tiled
        self.tiled_rows = experts * self.tiled
        self.rest_rows = experts * self.rest
        self.slots = experts * self.capacity
        self.message = (experts, FEATURE_BLOCKS * self.capacity, self.lanes)
        self.in_plane = experts // PLANES


def bring(source, place, done):
    copy = pltpu.make_async_copy(source, place, done)
    copy.start()
    return copy


def iota(shape, axis):
    return lax.broadcasted_iota(jnp.int32, shape, axis)


def dot(left, right):
    return jnp.dot(left, right, preferred_element_type=F32)


def dot_last(left, right):
    return lax.dot_general(left, right, (((1,), (1,)), ((), ())), preferred_element_type=F32)


def gelu_value(values):
    return 0.5 * values * (1.0 + lax.erf(values * ROOT_HALF))


def gelu_slope(values):
    return (
        0.5 * (1.0 + lax.erf(values * ROOT_HALF))
        + values * jnp.exp(-0.5 * values * values) * INV_ROOT_TAU
    )


def halves(values):
    high = values.astype(BF16)
    return high, (values - high.astype(F32)).astype(BF16)


def slot_parts(sizes):
    parts = []
    if sizes.tiled:
        parts.append((sizes.tiled, 0))
    if sizes.rest:
        parts.append((sizes.rest, sizes.tiled))
    return parts


def expansion(sizes, width):
    count = sizes.experts * width
    shape = (count, sizes.experts)
    first = iota(shape, 1) * width
    row = iota(shape, 0)
    return ((row >= first) & (row < first + width)).astype(BF16)


def expansion_across(sizes, width):
    count = sizes.experts * width
    shape = (sizes.experts, count)
    first = iota(shape, 0) * width
    column = iota(shape, 1)
    return ((column >= first) & (column < first + width)).astype(BF16)


def slots_by_token(sizes, table_across, gated, base=0):
    rows = sizes.rows
    names = (iota((sizes.experts, rows), 0) ^ base).astype(F32)
    first = table_across[0:1, :] == names
    second = table_across[1:2, :] == names
    chosen = jnp.where(first | second, 1.0, 0.0)
    earlier = (iota((rows, rows), 0) < iota((rows, rows), 1)).astype(BF16)
    rank = jnp.where(chosen > 0.0, dot(chosen.astype(BF16), earlier), -1.0).astype(BF16)
    if gated:
        gate = jnp.where(first, table_across[2:3, :], 0.0) + jnp.where(
            second, table_across[3:4, :], 0.0
        )
        high, low = halves(gate)
    ones, highs, lows = [], [], []
    for width, start in slot_parts(sizes):
        spread = expansion(sizes, width)
        ranks = dot(spread, rank)
        place = iota(ranks.shape, 0) % width + start
        here = ranks == place.astype(F32)
        if gated:
            highs.append(jnp.where(here, dot(spread, high), 0.0).astype(BF16))
            lows.append(jnp.where(here, dot(spread, low), 0.0).astype(BF16))
        else:
            ones.append(jnp.where(here, 1.0, 0.0).astype(BF16))
    if gated:
        return jnp.concatenate(highs, axis=0), jnp.concatenate(lows, axis=0)
    return jnp.concatenate(ones, axis=0)


def tokens_by_slot(sizes, table, gated):
    rows = sizes.rows
    names = iota((rows, sizes.experts), 1).astype(F32)
    first = table[:, 0:1] == names
    second = table[:, 1:2] == names
    chosen = jnp.where(first | second, 1.0, 0.0)
    earlier = (iota((rows, rows), 1) < iota((rows, rows), 0)).astype(BF16)
    rank = jnp.where(chosen > 0.0, dot(earlier, chosen.astype(BF16)), -1.0).astype(BF16)
    if gated:
        gate = jnp.where(first, table[:, 2:3], 0.0) + jnp.where(second, table[:, 3:4], 0.0)
        high, low = halves(gate)
    ones, highs, lows = [], [], []
    for width, start in slot_parts(sizes):
        spread = expansion_across(sizes, width)
        ranks = dot(rank, spread)
        place = iota(ranks.shape, 1) % width + start
        here = ranks == place.astype(F32)
        if gated:
            highs.append(jnp.where(here, dot(high, spread), 0.0).astype(BF16))
            lows.append(jnp.where(here, dot(low, spread), 0.0).astype(BF16))
        else:
            ones.append(jnp.where(here, 1.0, 0.0).astype(BF16))
    if gated:
        return jnp.concatenate(highs, axis=1), jnp.concatenate(lows, axis=1)
    return jnp.concatenate(ones, axis=1)


def rest_places(sizes, block):
    shape = (sizes.rest_rows * FEATURE_BLOCKS, sizes.rest_rows)
    return (iota(shape, 0) == iota(shape, 1) * FEATURE_BLOCKS + block).astype(BF16)


def rest_places_across(sizes, block):
    shape = (sizes.rest_rows, sizes.rest_rows * FEATURE_BLOCKS)
    return (iota(shape, 1) == iota(shape, 0) * FEATURE_BLOCKS + block).astype(BF16)


def all_rest_places(sizes, across):
    rows = sizes.rest_rows
    shape = (rows * FEATURE_BLOCKS, rows * FEATURE_BLOCKS)
    to, source = iota(shape, across), iota(shape, 1 - across)
    return ((to % FEATURE_BLOCKS) * rows + to // FEATURE_BLOCKS == source).astype(BF16)


def few_rest_rows(sizes):
    return sizes.rest_rows <= FEW_REST_ROWS and sizes.rest_rows % SLOT_TILE == 0


def write_pieces(sizes, pieces, block_values):
    tile, each = sizes.tiled, sizes.experts // len(pieces)
    rest, others = None, []
    for block in range(FEATURE_BLOCKS):
        values = block_values(block)
        if tile:
            for number, piece in enumerate(pieces):
                rows = values[number * each * tile : (number + 1) * each * tile].astype(BF16)
                piece[:, block * tile : (block + 1) * tile, :] = rows.reshape(
                    each, tile, sizes.lanes
                )
        if sizes.rest:
            other = values[sizes.tiled_rows :].astype(BF16)
            if few_rest_rows(sizes):
                others.append(other)
            else:
                part = dot(rest_places(sizes, block), other)
                rest = part if rest is None else rest + part
    if others:
        rest = dot(all_rest_places(sizes, 0), jnp.concatenate(others, axis=0))
    if sizes.rest:
        first, each_rest = FEATURE_BLOCKS * tile, FEATURE_BLOCKS * sizes.rest
        for number, piece in enumerate(pieces):
            rows = rest[number * each * each_rest : (number + 1) * each * each_rest]
            piece[:, first:, :] = rows.reshape(each, each_rest, sizes.lanes).astype(BF16)


def write_message(sizes, message, block_values):
    write_pieces(sizes, [message], block_values)


def read_rest(sizes, message):
    if not sizes.rest:
        return None
    first = FEATURE_BLOCKS * sizes.tiled
    rows = message[:, first:, :].astype(F32).reshape(sizes.rest_rows * FEATURE_BLOCKS, sizes.lanes)
    rows = rows.astype(BF16)
    if few_rest_rows(sizes):
        rows = dot(all_rest_places(sizes, 1), rows).astype(BF16)
    return rows


def read_block(sizes, message, rest, block):
    parts = []
    if sizes.tiled:
        parts.append(
            message[:, block * sizes.tiled : (block + 1) * sizes.tiled, :].reshape(
                sizes.tiled_rows, sizes.lanes
            )
        )
    if sizes.rest and few_rest_rows(sizes):
        parts.append(rest[block * sizes.rest_rows : (block + 1) * sizes.rest_rows])
    elif sizes.rest:
        parts.append(dot(rest_places_across(sizes, block), rest).astype(BF16))
    return jnp.concatenate(parts, axis=0)


def span(sizes, block):
    return slice(block * sizes.lanes, (block + 1) * sizes.lanes)


def inverse_rms(sizes, read):
    total = jnp.zeros((sizes.rows, 1), F32)
    for block in range(FEATURE_BLOCKS):
        wide = read(block).astype(F32)
        total = total + jnp.sum(wide * wide, axis=1, keepdims=True)
    return lax.rsqrt(total / sizes.features + EPSILON)


def cotangent_kernel(sizes, pick, clip, across, *planes):
    send_weighted(sizes, clip, across, planes, pick[1])


def regroup_kernel(sizes, *refs):
    planes, places = refs[:PLANES], refs[PLANES:]
    for number, place in enumerate(places):
        for plane_number, plane in enumerate(planes):
            place[plane_number] = plane[number]


def far_kernel(*refs):
    *places, plane = refs
    for number, place in enumerate(places):
        plane[number] = place[PLANES - 1]


def send_normed(sizes, carried, across, message):
    scale = inverse_rms(sizes, lambda block: carried[:, span(sizes, block)])
    select = slots_by_token(sizes, across[...], False)

    def values(block):
        normed = (carried[:, span(sizes, block)].astype(F32) * scale).astype(BF16)
        return dot(select, normed)

    write_message(sizes, message, values)


def send_weighted(sizes, incoming, across, pieces, base=0):
    high, low = slots_by_token(sizes, across[...], True, base)

    both = jnp.concatenate([high, low], axis=1)

    def values(block):
        rows = incoming[:, span(sizes, block)]
        return dot(both, jnp.concatenate([rows, rows], axis=0))

    write_pieces(sizes, pieces, values)


def middle_kernel(sizes, before, answer, table, across, carried, message):
    both = jnp.concatenate(tokens_by_slot(sizes, table[...], True), axis=0)
    rest = read_rest(sizes, answer)
    for block in range(FEATURE_BLOCKS):
        rows = read_block(sizes, answer, rest, block)
        parts = dot(both, rows)
        mixed = before[:, span(sizes, block)].astype(F32) + (
            parts[: sizes.rows] + parts[sizes.rows :]
        )
        carried[:, span(sizes, block)] = mixed.astype(BF16)
    send_normed(sizes, carried, across, message)


def norm_back(sizes, carried, incoming, answer, table, result, upstream, copies=()):
    select = tokens_by_slot(sizes, table[...], False)
    for copy in copies[:2]:
        copy.wait()
    rest = read_rest(sizes, answer)
    inner = jnp.zeros((sizes.rows, 1), F32)
    squares = jnp.zeros((sizes.rows, 1), F32)
    for block in range(FEATURE_BLOCKS):
        here = span(sizes, block)
        back = dot(select, read_block(sizes, answer, rest, block))
        wide = carried[:, here].astype(F32)
        upstream[:, here] = back
        inner = inner + jnp.sum(wide * back, axis=1, keepdims=True)
        squares = squares + jnp.sum(wide * wide, axis=1, keepdims=True)
    scale = lax.rsqrt(squares / sizes.features + EPSILON)
    pull = scale * scale * scale * (inner / sizes.features)
    for copy in copies[2:]:
        copy.wait()
    for block in range(FEATURE_BLOCKS):
        here = span(sizes, block)
        wide = carried[:, here].astype(F32)
        result[:, here] = (
            incoming[:, here].astype(F32) + (scale * upstream[:, here] - wide * pull)
        ).astype(BF16)


def hold_kernel(pick, grad, far, whole, done):
    @pl.when(pick[0] != 0)
    def _():
        copies = [bring(far, whole.at[0], done.at[0]), bring(grad, whole.at[1], done.at[1])]
        for copy in copies:
            copy.wait()


def assemble_kernel(pick, far, held, whole, done):
    @pl.when(pick[0] == 0)
    def _():
        bring(far, whole.at[1], done.at[0]).wait()


def last_kernel(
    sizes, pick, before, incoming, answer_far, table, held, result_out, whole,
    upstream, clip, grad, answer, result, done,
):
    copies = [
        bring(answer_far, answer, done.at[0]),
        bring(before, clip, done.at[1]),
        bring(incoming, grad, done.at[2]),
    ]
    norm_back(sizes, clip, grad, answer, table, result, upstream, copies)

    leaving = bring(result, result_out, done.at[4])

    @pl.when(pick[0] == 0)
    def _():
        bring(result, whole.at[0], done.at[3]).wait()

    leaving.wait()


def turn_kernel(sizes, carried, incoming, answer, table, across, result, message, upstream):
    norm_back(sizes, carried, incoming, answer, table, result, upstream)
    send_weighted(sizes, result, across, [message])


def through_up(sizes, received, up):
    rest = read_rest(sizes, received)
    hidden = jnp.zeros((sizes.slots, sizes.hidden), F32)
    for block in range(FEATURE_BLOCKS):
        rows = read_block(sizes, received, rest, block)
        hidden = hidden + dot(rows, up[span(sizes, block), :])
    return hidden


def through_down_back(sizes, received, down):
    rest = read_rest(sizes, received)
    back = jnp.zeros((sizes.slots, sizes.hidden), F32)
    for block in range(FEATURE_BLOCKS):
        rows = read_block(sizes, received, rest, block)
        back = back + dot_last(rows, down[:, span(sizes, block)])
    return back


def back_message(sizes, back_hidden, up, message):
    write_message(sizes, message, lambda block: dot_last(back_hidden, up[span(sizes, block), :]))


def forward_kernel(sizes, received, up, down, hidden_out, activated_out, message):
    hidden = through_up(sizes, received, up)
    hidden_out[...] = hidden
    activated = gelu_value(hidden).astype(BF16)
    activated_out[...] = activated
    write_message(sizes, message, lambda block: dot(activated, down[:, span(sizes, block)]))


def hidden_back_kernel(sizes, pick, down, *refs):
    count, last = sizes.in_plane, PLANES - 1
    places, far, (back_out, received, here, done) = refs[:count], refs[count], refs[count + 1 :]
    copies = []
    for number, place in enumerate(places):
        first = number * PLANES
        copies += [
            pltpu.make_async_copy(
                place.at[pl.ds(0, last)], here.at[pl.ds(first, last)], done.at[number]
            ),
            pltpu.make_async_copy(far.at[number], here.at[first + last], done.at[count + number]),
        ]
    for copy in copies:
        copy.start()
    for copy in copies:
        copy.wait()
    for sender in range(sizes.experts):
        partner = pick[1] ^ sender
        plane = partner // count
        received[sender] = here[(partner % count) * PLANES + (plane ^ plane // 2)]
    back_out[...] = through_down_back(sizes, received, down)


def turn_expert_kernel(sizes, received, back, up, activated_out, message):
    hidden = through_up(sizes, received, up)
    activated_out[...] = gelu_value(hidden).astype(BF16)
    back_hidden = (back[...] * gelu_slope(hidden)).astype(BF16)
    back_message(sizes, back_hidden, up, message)


def backward_kernel(sizes, received, hidden, up, down, message):
    slope = gelu_slope(hidden[...])
    back = through_down_back(sizes, received, down)
    back_message(sizes, (back * slope).astype(BF16), up, message)


def choose(pick, wanted, sources, places, semaphores):
    count = len(places)

    def begin(chosen):
        for number in range(count):
            pltpu.make_async_copy(chosen[number], places[number], semaphores.at[number]).start()

    @pl.when(pick[0] == wanted)
    def _():
        begin(sources[:count])

    @pl.when(pick[0] != wanted)
    def _():
        begin(sources[count:])

    for number in range(count):
        pltpu.make_async_copy(sources[number], places[number], semaphores.at[number]).wait()


def weights_kernel(pick, up, down, up_other, down_other, up_0, down_0, up_1, down_1, done):
    mine, others = (up, down), (up_other, down_other)
    choose(pick, 0, mine + others + others + mine, (up_0, down_0, up_1, down_1), done)


def down_grad_kernel(sizes, pick, *refs):
    sources, result, here, done = refs[:8], refs[8], refs[9:13], refs[13]
    choose(pick, 0, sources, here, done)
    near, near_grad, far, far_grad = here
    rest_near, rest_far = read_rest(sizes, near_grad), read_rest(sizes, far_grad)
    over_rows = (((0,), (0,)), ((), ()))
    for block in range(FEATURE_BLOCKS):
        rows_near = read_block(sizes, near_grad, rest_near, block)
        rows_far = read_block(sizes, far_grad, rest_far, block)
        total = lax.dot_general(near[...], rows_near, over_rows, preferred_element_type=F32)
        total = total + lax.dot_general(far[...], rows_far, over_rows, preferred_element_type=F32)
        result[:, span(sizes, block)] = total.astype(BF16)


TOOK = {
    "weights": 7, "send_tokens": 3, "send_cotangent": 4, "expert_forward": 6, "hidden_back": 5,
    "combine_send": 4, "expert_turn": 6, "norm_back_send": 5, "expert_backward": 6,
    "down_grad": 11, "norm_back_last": 6, "hold": 1, "assemble": 1, "regroup": 2, "far_plane": 1,
}
FLOPS_PER_MICROSECOND = 1_150_000_000


VMEM = pl.BlockSpec(memory_space=pltpu.VMEM)
SMEM = pl.BlockSpec(memory_space=pltpu.SMEM)
HBM = pl.BlockSpec(memory_space=pltpu.HBM)


def call(
    kernel, name, operands, outs, scratch=(), specs=None, out_specs=None, aliases=None,
    vmem=VMEM_BYTES,
):
    return pl.pallas_call(
        kernel,
        name=name,
        in_specs=specs or [VMEM] * len(operands),
        out_specs=out_specs or [VMEM] * len(outs),
        out_shape=[
            jax.ShapeDtypeStruct(*out) if isinstance(out, tuple) else out for out in outs
        ],
        scratch_shapes=list(scratch),
        input_output_aliases=aliases or {},
        cost_estimate=pl.CostEstimate(
            flops=TOOK[name] * FLOPS_PER_MICROSECOND, transcendentals=0, bytes_accessed=0
        ),
        compiler_params=pltpu.CompilerParams(vmem_limit_bytes=vmem),
    )(*operands)


def exchange(message):
    return lax.all_to_all(message, "expert", split_axis=0, concat_axis=0, tiled=True)


def to_partner(piece, number):
    if number == 0:
        return piece
    count = lax.axis_size("expert")
    return lax.ppermute(piece, "expert", [(source, source ^ number) for source in range(count)])


def shards(tokens, cotangent, expert_ids, gate_prob, up_weight, down_weight):
    core = lax.axis_index("pipe")
    rows, features = tokens.shape[1], tokens.shape[2]
    hidden = up_weight.shape[3]
    sizes = Sizes(lax.axis_size("expert"), rows, features, hidden)
    swap = [(0, 1), (1, 0)]
    pick = jnp.stack([core, lax.axis_index("expert")]).astype(jnp.int32)

    tables = jnp.concatenate([expert_ids[0].astype(F32), gate_prob[0]], axis=-1).swapaxes(1, 2)
    mine = lax.dynamic_index_in_dim(tables, core, 0, keepdims=False)
    theirs = lax.dynamic_index_in_dim(tables, 1 - core, 0, keepdims=False)
    theirs = lax.ppermute(theirs, "pipe", swap)
    clip = lax.dynamic_index_in_dim(tokens, core, 0, keepdims=False)
    clip_grad = lax.dynamic_index_in_dim(cotangent, core, 0, keepdims=False)
    across_0 = jnp.where(core == 0, mine, theirs)
    across_1 = jnp.where(core == 0, theirs, mine)
    table_0, table_1 = across_0.T, across_1.T
    up, down, theirs = lax.optimization_barrier((up_weight[0, 0], down_weight[0, 0], theirs))
    up_other = lax.ppermute(up, "pipe", swap)
    down_other = lax.ppermute(down, "pipe", swap)

    upstream_scratch = pltpu.VMEM((rows, features), F32)
    message = (sizes.message, BF16)
    home_rows = ((rows, features), BF16)
    activated = ((sizes.slots, hidden), BF16)
    wide_hidden = ((sizes.slots, hidden), F32)
    rows_scratch = pltpu.VMEM(*home_rows)
    up_shape, down_shape = ((features, hidden), BF16), ((hidden, features), BF16)

    def kernel(body, *more):
        return functools.partial(body, sizes, *more)

    def done(count):
        return pltpu.SemaphoreType.DMA((count,))

    up_0, down_0, up_1, down_1 = call(
        weights_kernel, "weights", [pick, up, down, up_other, down_other],
        [up_shape, down_shape] * 2, [done(4)], [SMEM] + [HBM] * 4, [HBM] * 4,
    )
    (out_0,) = call(kernel(send_normed), "send_tokens", [clip, across_0], [message])
    across_1_late, _, _ = lax.optimization_barrier((across_1, out_0, up_1))
    in_0 = exchange(out_0)
    plane = ((sizes.in_plane,) + sizes.message[1:], BF16)
    place = ((PLANES,) + sizes.message[1:], BF16)
    planes = call(
        kernel(cotangent_kernel), "send_cotangent", [pick, clip_grad, across_1_late],
        [plane] * PLANES, (), [SMEM, VMEM, VMEM],
    )
    last = PLANES - 1
    planes = [planes[number ^ number // 2] for number in range(PLANES)]
    near = [
        to_partner(planes[number], (number ^ number // 2) * sizes.in_plane)
        for number in range(last)
    ]
    hidden_0, activated_0, answer_0 = call(
        kernel(forward_kernel), "expert_forward", [in_0, up_0, down_0],
        [wide_hidden, activated, message],
    )
    *near, answer_0 = lax.optimization_barrier((*near, answer_0))
    returned_0 = exchange(answer_0)
    places = call(
        kernel(regroup_kernel), "regroup", near + [planes[last]], [place] * sizes.in_plane
    )
    places = [to_partner(piece, number) for number, piece in enumerate(places)]
    (far,) = call(far_kernel, "far_plane", places, [plane])
    _, returned_0 = lax.optimization_barrier((far, returned_0))
    far = to_partner(far, (last ^ last // 2) * sizes.in_plane)
    carried_1, out_1 = call(
        kernel(middle_kernel), "combine_send", [clip, returned_0, table_0, across_1],
        [home_rows, message],
    )
    far, out_1 = lax.optimization_barrier((far, out_1))
    in_1 = exchange(out_1)
    back_1, grad_in_1 = call(
        kernel(hidden_back_kernel), "hidden_back", [pick, down_1] + places + [far],
        [wide_hidden, message], [pltpu.VMEM(*message), done(2 * sizes.in_plane)],
        [SMEM, VMEM] + [HBM] * (sizes.in_plane + 1),
    )
    activated_1, picks_1 = call(
        kernel(turn_expert_kernel), "expert_turn", [in_1, back_1, up_1], [activated, message]
    )
    back_home_1 = exchange(picks_1)
    grad_1, grad_out_0 = call(
        kernel(turn_kernel), "norm_back_send",
        [carried_1, clip_grad, back_home_1, table_1, across_0],
        [home_rows, message], [upstream_scratch],
    )
    grad_in_0 = exchange(grad_out_0)
    (picks_0,) = call(
        kernel(backward_kernel), "expert_backward", [grad_in_0, hidden_0, up_0, down_0], [message]
    )
    back_home_0 = exchange(picks_0)

    to_first, to_second = [(1, 0)], [(0, 1)]
    operands = []
    for near, way in (
        ([activated_0, grad_in_0], to_first), ([activated_1, grad_in_1], to_second)
    ):
        operands += near + [lax.ppermute(array, "pipe", way) for array in near]
    (down_grad,) = call(
        kernel(down_grad_kernel), "down_grad", [pick] + operands, [((hidden, features), BF16)],
        [pltpu.VMEM(*activated), pltpu.VMEM(*message)] * 2 + [pltpu.SemaphoreType.DMA((4,))],
        [SMEM] + [HBM] * 8,
    )
    far_1 = lax.ppermute(grad_1, "pipe", to_second)
    held = (tokens.shape, BF16)
    (input_grad,) = call(
        hold_kernel, "hold", [pick, grad_1, far_1], [held], [done(2)], [SMEM, HBM, HBM], [HBM]
    )
    down_grad, input_grad, back_home_0 = lax.optimization_barrier(
        (down_grad, input_grad, back_home_0)
    )
    grad_0, input_grad = call(
        kernel(last_kernel), "norm_back_last",
        [pick, clip, grad_1, back_home_0, table_0, input_grad], [home_rows, held],
        [upstream_scratch, rows_scratch, rows_scratch, pltpu.VMEM(*message), rows_scratch, done(5)],
        [SMEM, HBM, HBM, HBM, VMEM, HBM], [HBM, HBM], {5: 1}, WHOLE_VMEM_BYTES,
    )
    far_0 = lax.ppermute(grad_0, "pipe", to_first)
    (input_grad,) = call(
        assemble_kernel, "assemble", [pick, far_0, input_grad], [held], [done(1)],
        [SMEM, HBM, HBM], [HBM], {2: 0},
    )
    return input_grad[None], down_grad[None, None]


def solution(mesh):
    placed = (
        P(None, "expert", None),
        P(None, "expert", None),
        P("pipe", None, "expert", None),
        P("pipe", None, "expert", None),
        P("pipe", "expert", None, None),
        P("pipe", "expert", None, None),
    )
    return jax.shard_map(
        shards,
        mesh=mesh,
        in_specs=placed,
        out_specs=(P("pipe", None, "expert", None), P("pipe", "expert", None, None)),
        check_vma=False,
    )
```
